32 devices in a mesh: chan: 16 (over z, x, core), stn: 2 (over y).
Axes of the slice: x: 2, y: 2, z: 4, core: 2. Of those that a mesh axis runs over, the one named last changes fastest.
Arguments:
- voltages: bfloat16 [16, 2, 256, 512], P(None, None, ('stn', 'chan')), may hold values from -6 to 6
- phase_index: int32 [256], P(('stn', 'chan')), may hold values from 0 to 1023
- int_lengths: int32 [4], replicated, may hold values from 1 to 192, 512 in all
- beam_weights: bfloat16 [2, 256, 256], replicated, may hold values from -0.375 to 0.375
Outputs:
- visibilities: bfloat16 [2, 2, 4, 16, 2, 128, 128], P('stn', None, None, 'chan')
- beam_power: float32 [4, 16, 256], P(None, 'chan', 'stn')
The draws below stay inside these ranges and needn't reach their ends.
Inputs may be any that keep to these rules, and one draw needn't show every extreme that they name: `int_lengths`: 4 integration lengths summing to 512; the longest is exactly 192.
All inputs are finite; a program needn't handle non-finite values.
Results may differ from the reference program's by a relative error of at most 0.0055.
Values may be sent and summed in bfloat16 or wider, within the bound.
No kernel may reach another device: no remote copies, remote signals or barrier semaphores. Data moves between devices by JAX's collectives and lax.ppermute only.
A program may use at most 64 MiB of HBM per device.

```python
import math
import jax
import jax.numpy as jnp
import numpy as np
from jax import lax

SAMPLES = 512
INTEG = 4
MOST = 192
BLK = 128
BEAMS = 256
PHASES = 1024
CHANNELS = 16
INPUTS = 256
PAIRS_DEV = 2
N_STN = 2


def touch_ends(values, stream_key, smallest, top_value):
    longest = values.shape.index(max(values.shape))
    spots = []
    for shift in (0, 1):
        where = [jax.random.randint(jax.random.fold_in(stream_key, axis), (), 0, length) for axis, length in enumerate(values.shape)]
        where[longest] = (where[longest] + shift) % values.shape[longest]
        spots.append(tuple(where))
    return values.at[spots[0]].set(smallest).at[spots[1]].set(top_value)


def block_scale(rng, extent, cuts, smallest, top_value):
    level = 1.0
    for dim, blocks in cuts:
        steps = jax.random.uniform(jax.random.fold_in(jax.random.fold_in(rng, 6), dim), (blocks,), jnp.float32, smallest / len(cuts), top_value / len(cuts))
        level = level * jnp.repeat(jnp.exp(steps), extent[dim] // blocks).reshape((-1,) + (1,) * (len(extent) - 1 - dim))
    return level


def length_profile(amount, total, limit, lean):
    weights = [(1 << 20) // math.isqrt(standing ** lean) + 1 for standing in range(2, amount + 1)]
    spare, holding = total - limit - (amount - 1), [1] * (amount - 1)
    while spare > 0:
        candidates = [i for i in range(amount - 1) if holding[i] < limit]
        whole, budget = sum([weights[i] for i in candidates]), spare
        for i in candidates:
            extra = min(limit - holding[i], max(1, budget * weights[i] // whole), spare)
            holding[i] = holding[i] + extra
            spare = spare - extra
    return np.array([limit] + holding)


def ragged(own_key, number_of, total, most, slope):
    if number_of == 2:
        one = jax.random.randint(own_key, (), max(1, total - most), min(most, total - 1) + 1)
        return jnp.stack([one, total - one])
    tallies = jnp.asarray(length_profile(number_of, total, most, slope), jnp.int32)
    pairs = (number_of - 1) // 2
    giver, receiver = tallies[1:1 + 2 * pairs:2], tallies[2:2 + 2 * pairs:2]
    margin = jnp.minimum(giver - 1, most - receiver)
    passed = jax.random.randint(jax.random.fold_in(own_key, 1), (pairs,), 0, 1 << 20) % (margin + 1)
    tallies = tallies.at[1:1 + 2 * pairs:2].set(giver - passed).at[2:2 + 2 * pairs:2].set(receiver + passed)
    return tallies[jax.random.permutation(jax.random.fold_in(own_key, 2), number_of)]


def bell_draw(own_key, extent, spread, reach, pieces=(), kind=jnp.bfloat16):
    entries = spread * jax.random.normal(own_key, extent, jnp.float32)
    if pieces:
        entries = entries * block_scale(own_key, extent, pieces, -0.22, 0.18)
    return jnp.clip(entries, -reach, reach).astype(kind)


def setup_inputs(seed: int = 0) -> dict:
    streams_of = jax.random.split(jax.random.key(seed), 5)
    voltages = bell_draw(streams_of[0], (CHANNELS, 2, INPUTS, SAMPLES), 1.0, 6.0, ((2, 32),))
    phase_index = touch_ends(jax.random.randint(streams_of[1], (INPUTS,), 0, PHASES), jax.random.fold_in(streams_of[1], 1), 0, PHASES - 1).astype(jnp.int32)
    int_lengths = ragged(streams_of[2], INTEG, SAMPLES, MOST, 0).astype(jnp.int32)
    beam_weights = bell_draw(streams_of[3], (2, BEAMS, INPUTS), INPUTS ** -0.5, 0.375)
    return {"voltages": voltages, "phase_index": phase_index, "int_lengths": int_lengths, "beam_weights": beam_weights}


full_turn = 2.0 * math.pi


def rotate(voltages, phase_index, channel):
    phase_turns = (channel[:, None] * phase_index[None, :]) % PHASES
    phase_angle = phase_turns.astype(jnp.float32) * (full_turn / PHASES)
    cosine = jnp.cos(phase_angle)[:, :, None]
    sine_part = jnp.sin(phase_angle)[:, :, None]
    real_in = voltages[:, 0].astype(jnp.float32)
    imag_in = voltages[:, 1].astype(jnp.float32)
    return jnp.stack([real_in * cosine + imag_in * sine_part, imag_in * cosine - real_in * sine_part], axis=1).astype(jnp.bfloat16)


def windows(block, starts, int_lengths):
    padded = jnp.pad(block, ((0, 0), (0, 0), (0, MOST)))
    in_range = jnp.arange(MOST, dtype=jnp.int32)
    result = []
    for period in range(INTEG):
        segment = lax.dynamic_slice_in_dim(padded, starts[period], MOST, 2)
        keep_mask = (in_range < int_lengths[period])[None, None, :]
        result.append(jnp.where(keep_mask, segment, jnp.zeros_like(segment)))
    return jnp.stack(result)


def correlate(own_parts, other, starts, int_lengths):
    padded = jnp.pad(other, ((0, 0), (0, 0), (0, MOST)))
    block_rows = own_parts.shape[2] // 2
    result = []
    for period in range(INTEG):
        segment = lax.dynamic_slice_in_dim(padded, starts[period], MOST, 2)
        products = jnp.einsum('cal,cbl->cab', own_parts[period].astype(jnp.float32), segment.astype(jnp.float32), precision=lax.Precision.HIGHEST)
        real_part = products[:, :block_rows, :block_rows] + products[:, block_rows:, block_rows:]
        imag_part = products[:, block_rows:, :block_rows] - products[:, :block_rows, block_rows:]
        inverse = 1.0 / int_lengths[period].astype(jnp.float32)
        result.append((jnp.stack([real_part, imag_part], axis=1) * inverse).astype(jnp.bfloat16))
    return jnp.stack(result)


def stack_weights(beam_weights, columns):
    weight_real = beam_weights[0][:, columns]
    weight_imag = beam_weights[1][:, columns]
    upper = jnp.concatenate([weight_real, -weight_imag], axis=1)
    lower = jnp.concatenate([weight_imag, weight_real], axis=1)
    return jnp.concatenate([upper, lower], axis=0)


def reference(voltages, phase_index, int_lengths, beam_weights):
    channel = jnp.arange(CHANNELS, dtype=jnp.int32)
    rotated = rotate(voltages, phase_index, channel)
    starts = (jnp.cumsum(int_lengths) - int_lengths).astype(jnp.int32)
    blocks = [rotated[:, :, station * BLK:(station + 1) * BLK, :].reshape(CHANNELS, 2 * BLK, SAMPLES) for station in range(N_STN)]
    vis_rows = []
    for station in range(N_STN):
        own_parts = windows(blocks[station], starts, int_lengths)
        slots = []
        for offset in range(PAIRS_DEV):
            slots.append(correlate(own_parts, blocks[(station + offset) % N_STN], starts, int_lengths))
        vis_rows.append(jnp.stack(slots))
    visibilities = jnp.stack(vis_rows)
    beam_total = jnp.zeros((CHANNELS, 2 * BEAMS, SAMPLES), jnp.float32)
    for station in range(N_STN):
        stacked = stack_weights(beam_weights, slice(station * BLK, (station + 1) * BLK))
        partial_beam = jnp.einsum('rk,ckt->crt', stacked.astype(jnp.float32), blocks[station].astype(jnp.float32), precision=lax.Precision.HIGHEST)
        beam_total = beam_total + lax.optimization_barrier(partial_beam.astype(jnp.bfloat16)).astype(jnp.float32)
    beam_total = beam_total.reshape(CHANNELS, 2, BEAMS, SAMPLES)
    power = beam_total[:, 0] ** 2 + beam_total[:, 1] ** 2
    sample_index = jnp.arange(SAMPLES, dtype=jnp.int32)[None, :]
    in_window = ((sample_index >= starts[:, None]) & (sample_index < (starts + int_lengths)[:, None])).astype(jnp.float32)
    beam_power = jnp.einsum('cbt,jt->jcb', power, in_window, precision=lax.Precision.HIGHEST)
    beam_power = beam_power / int_lengths.astype(jnp.float32)[:, None, None]
    return visibilities, beam_power
```

```python
import functools
import math

import jax
import jax.numpy as jnp
from jax import lax
from jax.experimental import pallas as pl
from jax.experimental.pallas import tpu as pltpu
from jax.sharding import PartitionSpec as P

PHASES = 1024
VMEM_BYTES = 32 * 1024 * 1024


def phasors(turns):
    quarter = PHASES // 4
    quadrant = (turns + quarter // 2) // quarter
    x = (turns - quadrant * quarter).astype(jnp.float32) * (2.0 * math.pi / PHASES)
    xx = x * x
    sine = x * (1.0 + xx * (-1.0 / 6 + xx * (1.0 / 120 + xx * (-1.0 / 5040 + xx * (1.0 / 362880)))))
    cosine = 1.0 + xx * (-0.5 + xx * (1.0 / 24 + xx * (-1.0 / 720 + xx * (1.0 / 40320))))
    odd = (quadrant % 2) == 1
    cos_out = jnp.where(odd, sine, cosine)
    sin_out = jnp.where(odd, cosine, sine)
    cos_out = jnp.where((quadrant == 1) | (quadrant == 2), -cos_out, cos_out)
    sin_out = jnp.where((quadrant == 2) | (quadrant == 3), -sin_out, sin_out)
    return cos_out, sin_out


def rotate_kernel(phase_ref, volt_ref, out_ref):
    channels, _, rows, samples = volt_ref.shape
    row = lax.broadcasted_iota(jnp.int32, (rows, 128), 0)
    channel = lax.broadcasted_iota(jnp.int32, (rows, 128), 1)
    step = jnp.zeros((rows, 128), jnp.int32)
    for r in range(rows):
        step = jnp.where(row == r, phase_ref[r], step)
    cosine, sine = phasors((step * channel) % PHASES)
    for c in range(channels):
        cos_c = cosine[:, c : c + 1]
        sin_c = sine[:, c : c + 1]
        real_in = volt_ref[c, 0].astype(jnp.float32)
        imag_in = volt_ref[c, 1].astype(jnp.float32)
        real_out = (real_in * cos_c + imag_in * sin_c).astype(jnp.bfloat16)
        imag_out = (imag_in * cos_c - real_in * sin_c).astype(jnp.bfloat16)
        for s in range(out_ref.shape[0]):
            out_ref[s, c, 0] = real_out
            out_ref[s, c, 1] = imag_out


def rotate(voltages, phase_index, copies):
    return pl.pallas_call(
        rotate_kernel,
        out_shape=jax.ShapeDtypeStruct((copies, *voltages.shape), jnp.bfloat16),
        in_specs=[
            pl.BlockSpec(memory_space=pltpu.SMEM),
            pl.BlockSpec(memory_space=pltpu.VMEM),
        ],
        out_specs=pl.BlockSpec(memory_space=pltpu.VMEM),
        compiler_params=pltpu.CompilerParams(vmem_limit_bytes=VMEM_BYTES),
    )(phase_index, voltages)


def dot_nt(a, b):
    return lax.dot_general(a, b, (((1,), (1,)), ((), ())), preferred_element_type=jnp.float32)


def finish_kernel(length_ref, weight_ref, blocks_ref, vis_ref, power_ref):
    stations, twice, samples = blocks_ref.shape
    half = twice // 2
    integs = length_ref.shape[0]
    slots = vis_ref.shape[1]
    share = power_ref.shape[2]
    station = lax.axis_index("stn")

    sample = lax.broadcasted_iota(jnp.int32, (1, samples), 1)
    masks = []
    start = jnp.int32(0)
    for j in range(integs):
        end = start + length_ref[j]
        masks.append(jnp.where((sample >= start) & (sample < end), 1.0, 0.0))
        start = end

    own = blocks_ref[station]
    for j in range(integs):
        part = own * masks[j].astype(jnp.bfloat16)
        inverse = 1.0 / jnp.full((1, half), length_ref[j], jnp.int32).astype(jnp.float32)
        for k in range(slots):
            other = own if k == 0 else blocks_ref[lax.rem(station + k, stations)]
            prod = dot_nt(part, other)
            real = prod[:half, :half] + prod[half:, half:]
            imag = prod[half:, :half] - prod[:half, half:]
            vis_ref[0, k, j, 0, 0] = (real * inverse).astype(jnp.bfloat16)
            vis_ref[0, k, j, 0, 1] = (imag * inverse).astype(jnp.bfloat16)

    rows = pl.ds(pl.multiple_of(station * share, share), share)
    beam = jnp.zeros((2 * share, samples), jnp.float32)
    for b in range(stations):
        w_real = weight_ref[0, rows, b * half : (b + 1) * half]
        w_imag = weight_ref[1, rows, b * half : (b + 1) * half]
        stacked = jnp.concatenate(
            [
                jnp.concatenate([w_real, -w_imag], axis=1),
                jnp.concatenate([w_imag, w_real], axis=1),
            ],
            axis=0,
        )
        beam = beam + jnp.dot(stacked, blocks_ref[b], preferred_element_type=jnp.float32)
    power = beam[:share] * beam[:share] + beam[share:] * beam[share:]
    high = power.astype(jnp.bfloat16)
    low = (power - high.astype(jnp.float32)).astype(jnp.bfloat16)
    window = jnp.concatenate(
        masks + [jnp.zeros((16 - integs, samples), jnp.float32)], axis=0
    ).astype(jnp.bfloat16)
    summed = dot_nt(window, high) + dot_nt(window, low)
    for j in range(integs):
        count = jnp.full((1, share), length_ref[j], jnp.int32).astype(jnp.float32)
        power_ref[j] = summed[j : j + 1] / count


def finish(int_lengths, beam_weights, blocks, slots):
    stations, twice, samples = blocks.shape
    integs = int_lengths.shape[0]
    half = twice // 2
    return pl.pallas_call(
        finish_kernel,
        out_shape=(
            jax.ShapeDtypeStruct((1, slots, integs, 1, 2, half, half), jnp.bfloat16),
            jax.ShapeDtypeStruct((integs, 1, beam_weights.shape[1] // stations), jnp.float32),
        ),
        in_specs=[
            pl.BlockSpec(memory_space=pltpu.SMEM),
            pl.BlockSpec(memory_space=pltpu.VMEM),
            pl.BlockSpec(memory_space=pltpu.VMEM),
        ],
        out_specs=(
            pl.BlockSpec(memory_space=pltpu.VMEM),
            pl.BlockSpec(memory_space=pltpu.VMEM),
        ),
        compiler_params=pltpu.CompilerParams(vmem_limit_bytes=VMEM_BYTES),
    )(int_lengths, beam_weights, blocks)


def local(voltages, phase_index, int_lengths, beam_weights):
    stations = lax.axis_size("stn")
    channels, parts, rows, samples = voltages.shape
    sent = rotate(voltages, phase_index, stations)
    got = lax.all_to_all(
        sent.reshape(stations * channels, parts, rows, samples),
        ("stn", "chan"),
        split_axis=0,
        concat_axis=0,
        tiled=True,
    )
    blocks = (
        got.reshape(stations, channels, parts, rows, samples)
        .transpose(0, 2, 1, 3, 4)
        .reshape(stations, parts * channels * rows, samples)
    )
    return finish(int_lengths, beam_weights, blocks, stations // 2 + 1)


def solution(mesh):
    return jax.shard_map(
        local,
        mesh=mesh,
        in_specs=(P(None, None, ("stn", "chan"), None), P(("stn", "chan")), P(), P()),
        out_specs=(P("stn", None, None, "chan", None, None, None), P(None, "chan", "stn")),
        check_vma=False,
    )
```

```python
import functools
import math

import jax
import jax.numpy as jnp
from jax import lax
from jax.experimental import pallas as pl
from jax.experimental.pallas import tpu as pltpu
from jax.sharding import PartitionSpec as P

PHASES = 1024
VMEM_BYTES = 32 * 1024 * 1024
IN_VMEM = pl.BlockSpec(memory_space=pltpu.VMEM)
IN_SMEM = pl.BlockSpec(memory_space=pltpu.SMEM)


def params():
    return pltpu.CompilerParams(vmem_limit_bytes=VMEM_BYTES)


def phasors(turns):
    quarter = PHASES // 4
    quadrant = (turns + quarter // 2) // quarter
    x = (turns - quadrant * quarter).astype(jnp.float32) * (2.0 * math.pi / PHASES)
    xx = x * x
    sine = x * (1.0 + xx * (-1.0 / 6 + xx * (1.0 / 120 + xx * (-1.0 / 5040 + xx * (1.0 / 362880)))))
    cosine = 1.0 + xx * (-0.5 + xx * (1.0 / 24 + xx * (-1.0 / 720 + xx * (1.0 / 40320))))
    odd = (quadrant % 2) == 1
    cos_out = jnp.where(odd, sine, cosine)
    sin_out = jnp.where(odd, cosine, sine)
    cos_out = jnp.where((quadrant == 1) | (quadrant == 2), -cos_out, cos_out)
    sin_out = jnp.where((quadrant == 2) | (quadrant == 3), -sin_out, sin_out)
    return cos_out, sin_out


def rotate_kernel(step_ref, volt_ref, kept_ref, given_ref):
    channels, _, rows, samples = volt_ref.shape
    me = lax.axis_index("chan")
    slot = lax.broadcasted_iota(jnp.int32, step_ref.shape, 1)
    cosine, sine = phasors((step_ref[...] * jnp.bitwise_xor(slot, me)) % PHASES)
    for k in range(channels):
        c = jnp.bitwise_xor(me, k)
        cos_c = cosine[:, k : k + 1]
        sin_c = sine[:, k : k + 1]
        real_in = volt_ref[c, 0].astype(jnp.float32)
        imag_in = volt_ref[c, 1].astype(jnp.float32)
        out_ref = given_ref if k % 2 else kept_ref
        out_ref[k // 2, 0] = (real_in * cos_c + imag_in * sin_c).astype(jnp.bfloat16)
        out_ref[k // 2, 1] = (imag_in * cos_c - real_in * sin_c).astype(jnp.bfloat16)


def rotate(voltages, phase_index):
    channels, parts, rows, samples = voltages.shape
    step = jnp.broadcast_to(phase_index[:, None], (rows, 128 * pl.cdiv(channels, 128)))
    half = jax.ShapeDtypeStruct((channels // 2, parts, rows, samples), jnp.bfloat16)
    return pl.pallas_call(
        rotate_kernel,
        out_shape=(half, half),
        in_specs=[IN_VMEM, IN_VMEM],
        out_specs=(IN_VMEM, IN_VMEM),
        compiler_params=params(),
    )(step, voltages)


def prepare_kernel(length_ref, weight_ref, window_ref, inverse_ref, stacked_ref):
    integs = length_ref.shape[0]
    stations, twice, width = stacked_ref.shape
    share, half = twice // 2, width // 2
    sample = lax.broadcasted_iota(jnp.int32, (1, window_ref.shape[1]), 1)
    window_ref[...] = jnp.zeros(window_ref.shape, jnp.float32)
    start = jnp.int32(0)
    for j in range(integs):
        end = start + length_ref[j]
        window_ref[j : j + 1] = jnp.where((sample >= start) & (sample < end), 1.0, 0.0)
        inverse_ref[j : j + 1] = 1.0 / jnp.full((1, inverse_ref.shape[1]), length_ref[j]).astype(
            jnp.float32
        )
        start = end
    rows = pl.ds(pl.multiple_of(lax.axis_index("stn") * share, share), share)
    for b in range(stations):
        w_real = weight_ref[0, rows, b * half : (b + 1) * half]
        w_imag = weight_ref[1, rows, b * half : (b + 1) * half]
        stacked_ref[b, :share, :half] = w_real
        stacked_ref[b, :share, half:] = -w_imag
        stacked_ref[b, share:, :half] = w_imag
        stacked_ref[b, share:, half:] = w_real


def prepare(int_lengths, beam_weights, stations, block, samples):
    share = beam_weights.shape[1] // stations
    return pl.pallas_call(
        prepare_kernel,
        out_shape=(
            jax.ShapeDtypeStruct((16, samples), jnp.float32),
            jax.ShapeDtypeStruct((int_lengths.shape[0], 128), jnp.float32),
            jax.ShapeDtypeStruct((stations, 2 * share, 2 * block), jnp.bfloat16),
        ),
        in_specs=[IN_SMEM, IN_VMEM],
        out_specs=(IN_VMEM, IN_VMEM, IN_VMEM),
        compiler_params=params(),
    )(int_lengths, beam_weights)


def dot_nt(a, b):
    return lax.dot_general(a, b, (((1,), (1,)), ((), ())), preferred_element_type=jnp.float32)


def finish_kernel(layout, window_ref, inverse_ref, stacked_ref, *refs):
    pieces, (vis_ref, power_ref, blocks_ref) = refs[:-3], refs[-3:]
    stations, parts, channels, rows, samples = blocks_ref.shape
    twice = parts * channels * rows
    half = twice // 2
    _, slots, integs = vis_ref.shape[:3]
    share = power_ref.shape[2]
    me = lax.axis_index("chan")
    station = lax.axis_index("stn")

    for piece_ref, (dy, offsets) in zip(pieces, layout):
        b = lax.rem(station + dy, stations)
        for i, offset in enumerate(offsets):
            source = jnp.bitwise_xor(me, offset)
            for part in range(parts):
                blocks_ref[b, part, source] = piece_ref[i, part]

    def block(b):
        return blocks_ref[b].astype(jnp.float32).reshape(twice, samples).astype(jnp.bfloat16)

    window = window_ref[...].astype(jnp.bfloat16)
    own = block(station)
    masked = jnp.concatenate([own * window[j : j + 1] for j in range(integs)], axis=0)
    for k in range(slots):
        other = own if k == 0 else block(lax.rem(station + k, stations))
        products = dot_nt(masked, other)
        for j in range(integs):
            prod = products[j * twice : (j + 1) * twice]
            inverse = inverse_ref[j : j + 1]
            real = prod[:half, :half] + prod[half:, half:]
            imag = prod[half:, :half] - prod[:half, half:]
            vis_ref[0, k, j, 0, 0] = (real * inverse).astype(jnp.bfloat16)
            vis_ref[0, k, j, 0, 1] = (imag * inverse).astype(jnp.bfloat16)

    beam = jnp.zeros((2 * share, samples), jnp.float32)
    for b in range(stations):
        beam = beam + jnp.dot(stacked_ref[b], block(b), preferred_element_type=jnp.float32)
    power = beam[:share] * beam[:share] + beam[share:] * beam[share:]
    high = power.astype(jnp.bfloat16)
    low = (power - high.astype(jnp.float32)).astype(jnp.bfloat16)
    summed = dot_nt(window, high) + dot_nt(window, low)
    for j in range(integs):
        power_ref[j] = summed[j : j + 1] * inverse_ref[j : j + 1, :share]


def finish(prepared, pieces, layout, slots, integs, share, block_shape):
    stations, parts, channels, rows, samples = block_shape
    half = channels * rows
    return pl.pallas_call(
        functools.partial(finish_kernel, layout),
        out_shape=(
            jax.ShapeDtypeStruct((1, slots, integs, 1, 2, half, half), jnp.bfloat16),
            jax.ShapeDtypeStruct((integs, 1, share), jnp.float32),
        ),
        in_specs=[IN_VMEM] * (len(prepared) + len(pieces)),
        out_specs=(IN_VMEM, IN_VMEM),
        scratch_shapes=[pltpu.VMEM(block_shape, jnp.bfloat16)],
        compiler_params=params(),
    )(*prepared, *pieces)


def exchanged(value, offset, dy):
    channels, stations = lax.axis_size("chan"), lax.axis_size("stn")
    if dy == 0:
        return lax.ppermute(value, "chan", [(c, c ^ offset) for c in range(channels)])
    pairs = [
        ((c ^ offset) * stations + (s + dy) % stations, c * stations + s)
        for c in range(channels)
        for s in range(stations)
    ]
    return lax.ppermute(value, ("chan", "stn"), pairs)


def local(voltages, phase_index, int_lengths, beam_weights):
    stations = lax.axis_size("stn")
    channels, parts, rows, samples = voltages.shape
    far = channels // 4
    kept, given = rotate(voltages, phase_index)
    prepared = prepare(int_lengths, beam_weights, stations, channels * rows, samples)

    both = jnp.stack([kept, exchanged(given, 1, 0)], axis=1)
    both = both.reshape(far, 2, 2, parts, rows, samples)
    arrived = [both[0]] + [exchanged(both[k], 4 * k, 0) for k in range(1, far)]

    def held(dx, ks):
        slabs = [arrived[k][dx] for k in ks]
        return slabs[0] if len(slabs) == 1 else jnp.concatenate(slabs, axis=0)

    every = tuple(range(far))
    pieces, layout = [], []
    for dy in range(1, stations):
        pieces.append(exchanged(held(1, (0,)), 2, dy))
        layout.append((1, dy, (0,)))
    pieces, arrived = lax.optimization_barrier((pieces, arrived))
    for dy in range(stations):
        for dx in range(2):
            ks = every[1:] if dx and dy else every
            piece = held(dx, ks)
            pieces.append(exchanged(piece, 2 * dx, dy) if dx or dy else piece)
            layout.append((dx, dy, ks))
    layout = [
        (dy, tuple(4 * k + 2 * dx + pair for k in ks for pair in range(2)))
        for dx, dy, ks in layout
    ]
    return finish(
        prepared,
        pieces,
        layout,
        stations // 2 + 1,
        int_lengths.shape[0],
        beam_weights.shape[1] // stations,
        (stations, parts, channels, rows, samples),
    )


def solution(mesh):
    return jax.shard_map(
        local,
        mesh=mesh,
        in_specs=(P(None, None, ("stn", "chan"), None), P(("stn", "chan")), P(), P()),
        out_specs=(P("stn", None, None, "chan", None, None, None), P(None, "chan", "stn")),
        check_vma=False,
    )
```

```python
import functools
import math

import jax
import jax.numpy as jnp
from jax import lax
from jax.experimental import pallas as pl
from jax.experimental.pallas import tpu as pltpu
from jax.sharding import PartitionSpec as P

PHASES = 1024
VMEM_BYTES = 32 * 1024 * 1024
IN_VMEM = pl.BlockSpec(memory_space=pltpu.VMEM)
IN_SMEM = pl.BlockSpec(memory_space=pltpu.SMEM)


def params():
    return pltpu.CompilerParams(vmem_limit_bytes=VMEM_BYTES)


def phasors(turns):
    quarter = PHASES // 4
    quadrant = (turns + quarter // 2) // quarter
    x = (turns - quadrant * quarter).astype(jnp.float32) * (2.0 * math.pi / PHASES)
    xx = x * x
    sine = x * (1.0 + xx * (-1.0 / 6 + xx * (1.0 / 120 + xx * (-1.0 / 5040 + xx * (1.0 / 362880)))))
    cosine = 1.0 + xx * (-0.5 + xx * (1.0 / 24 + xx * (-1.0 / 720 + xx * (1.0 / 40320))))
    odd = (quadrant % 2) == 1
    cos_out = jnp.where(odd, sine, cosine)
    sin_out = jnp.where(odd, cosine, sine)
    cos_out = jnp.where((quadrant == 1) | (quadrant == 2), -cos_out, cos_out)
    sin_out = jnp.where((quadrant == 2) | (quadrant == 3), -sin_out, sin_out)
    return cos_out, sin_out


def rotate_kernel(step_ref, volt_ref, kept_ref, given_ref):
    channels, _, rows, samples = volt_ref.shape
    me = lax.axis_index("chan")
    slot = lax.broadcasted_iota(jnp.int32, step_ref.shape, 1)
    cosine, sine = phasors((step_ref[...] * jnp.bitwise_xor(slot, me)) % PHASES)
    for k in range(channels):
        c = jnp.bitwise_xor(me, k)
        cos_c = cosine[:, k : k + 1]
        sin_c = sine[:, k : k + 1]
        real_in = volt_ref[c, 0]
        imag_in = volt_ref[c, 1]
        out_ref = given_ref if k % 2 else kept_ref
        out_ref[k // 2, 0] = (real_in * cos_c + imag_in * sin_c).astype(jnp.bfloat16)
        out_ref[k // 2, 1] = (imag_in * cos_c - real_in * sin_c).astype(jnp.bfloat16)


def rotate(voltages, phase_index):
    channels, parts, rows, samples = voltages.shape
    step = jnp.broadcast_to(phase_index[:, None], (rows, 128 * pl.cdiv(channels, 128)))
    half = jax.ShapeDtypeStruct((channels // 2, parts, rows, samples), jnp.bfloat16)
    return pl.pallas_call(
        rotate_kernel,
        out_shape=(half, half),
        in_specs=[IN_VMEM, IN_VMEM],
        out_specs=(IN_VMEM, IN_VMEM),
        compiler_params=params(),
    )(step, voltages.astype(jnp.float32))


def prepare_kernel(length_ref, weight_ref, window_ref, inverse_ref, stacked_ref):
    integs = length_ref.shape[0]
    stations, twice, width = stacked_ref.shape
    share, half = twice // 2, width // 2
    sample = lax.broadcasted_iota(jnp.int32, (1, window_ref.shape[1]), 1)
    window_ref[...] = jnp.zeros(window_ref.shape, jnp.float32)
    start = jnp.int32(0)
    for j in range(integs):
        end = start + length_ref[j]
        window_ref[j : j + 1] = jnp.where((sample >= start) & (sample < end), 1.0, 0.0)
        inverse_ref[j : j + 1] = 1.0 / jnp.full((1, inverse_ref.shape[1]), length_ref[j]).astype(
            jnp.float32
        )
        start = end
    rows = pl.ds(pl.multiple_of(lax.axis_index("stn") * share, share), share)
    for b in range(stations):
        w_real = weight_ref[0, rows, b * half : (b + 1) * half]
        w_imag = weight_ref[1, rows, b * half : (b + 1) * half]
        stacked_ref[b, :share, :half] = w_real
        stacked_ref[b, :share, half:] = -w_imag
        stacked_ref[b, share:, :half] = w_imag
        stacked_ref[b, share:, half:] = w_real


def prepare(int_lengths, beam_weights, stations, block, samples):
    share = beam_weights.shape[1] // stations
    return pl.pallas_call(
        prepare_kernel,
        out_shape=(
            jax.ShapeDtypeStruct((16, samples), jnp.float32),
            jax.ShapeDtypeStruct((int_lengths.shape[0], 128), jnp.float32),
            jax.ShapeDtypeStruct((stations, 2 * share, 2 * block), jnp.bfloat16),
        ),
        in_specs=[IN_SMEM, IN_VMEM],
        out_specs=(IN_VMEM, IN_VMEM, IN_VMEM),
        compiler_params=params(),
    )(int_lengths, beam_weights)


def dot_nt(a, b):
    return lax.dot_general(a, b, (((1,), (1,)), ((), ())), preferred_element_type=jnp.float32)


def assemble(pieces, layout, blocks_ref):
    me = lax.axis_index("chan")
    for piece_ref, (block, offsets) in zip(pieces, layout):
        for i, offset in enumerate(offsets):
            source = jnp.bitwise_xor(me, offset)
            for part in range(piece_ref.shape[1]):
                blocks_ref[block, part, source] = piece_ref[i, part]


def assembled(blocks_ref, block):
    _, parts, channels, rows, samples = blocks_ref.shape
    values = blocks_ref[block].astype(jnp.float32)
    return values.reshape(parts * channels * rows, samples).astype(jnp.bfloat16)


def correlate(own, other, window_ref, inverse_ref, vis_ref):
    integs = vis_ref.shape[2]
    twice = own.shape[0]
    half = twice // 2
    window = window_ref[...].astype(jnp.bfloat16)
    masked = jnp.concatenate([own * window[j : j + 1] for j in range(integs)], axis=0)
    products = dot_nt(masked, other)
    for j in range(integs):
        prod = products[j * twice : (j + 1) * twice]
        inverse = inverse_ref[j : j + 1]
        real = prod[:half, :half] + prod[half:, half:]
        imag = prod[half:, :half] - prod[:half, half:]
        vis_ref[0, 0, j, 0, 0] = (real * inverse).astype(jnp.bfloat16)
        vis_ref[0, 0, j, 0, 1] = (imag * inverse).astype(jnp.bfloat16)


def own_kernel(layout, window_ref, inverse_ref, stacked_ref, *refs):
    pieces, (vis_ref, own_ref, beam_ref, blocks_ref) = refs[:-4], refs[-4:]
    assemble(pieces, layout, blocks_ref)
    own = assembled(blocks_ref, 0)
    own_ref[...] = own
    correlate(own, own, window_ref, inverse_ref, vis_ref)
    beam_ref[...] = jnp.dot(
        stacked_ref[lax.axis_index("stn")], own, preferred_element_type=jnp.float32
    )


def other_kernel(layout, window_ref, inverse_ref, stacked_ref, own_ref, beam_ref, *refs):
    pieces, (vis_ref, power_ref, blocks_ref) = refs[:-4], refs[-3:]
    others = blocks_ref.shape[0]
    integs, _, share = power_ref.shape
    station = lax.axis_index("stn")
    slot = pl.program_id(0)

    @pl.when(slot == 0)
    def _():
        assemble(pieces, layout, blocks_ref)

    correlate(own_ref[...], assembled(blocks_ref, slot), window_ref, inverse_ref, vis_ref)

    @pl.when(slot == pl.num_programs(0) - 1)
    def _():
        beam = beam_ref[...]
        for b in range(others):
            weights = stacked_ref[lax.rem(station + b + 1, others + 1)]
            beam = beam + jnp.dot(
                weights, assembled(blocks_ref, b), preferred_element_type=jnp.float32
            )
        power = beam[:share] * beam[:share] + beam[share:] * beam[share:]
        high = power.astype(jnp.bfloat16)
        low = (power - high.astype(jnp.float32)).astype(jnp.bfloat16)
        window = window_ref[...].astype(jnp.bfloat16)
        summed = dot_nt(window, high) + dot_nt(window, low)
        for j in range(integs):
            power_ref[j] = summed[j : j + 1] * inverse_ref[j : j + 1, :share]


def finish(prepared, pieces, layout, slots, integs, share, block_shape):
    stations, parts, channels, rows, samples = block_shape
    half = channels * rows
    vis = jax.ShapeDtypeStruct((1, slots, integs, 1, 2, half, half), jnp.bfloat16)
    vis_block = (1, 1, integs, 1, 2, half, half)

    near = [(p, (0, o)) for p, (dy, o) in zip(pieces, layout) if dy == 0]
    vis, own, beam = pl.pallas_call(
        functools.partial(own_kernel, [place for _, place in near]),
        grid=(1,),
        out_shape=(
            vis,
            jax.ShapeDtypeStruct((2 * half, samples), jnp.bfloat16),
            jax.ShapeDtypeStruct((2 * share, samples), jnp.float32),
        ),
        in_specs=[IN_VMEM] * (len(prepared) + len(near)),
        out_specs=(
            pl.BlockSpec(vis_block, lambda k: (0, 0, 0, 0, 0, 0, 0)),
            IN_VMEM,
            IN_VMEM,
        ),
        scratch_shapes=[pltpu.VMEM((1, *block_shape[1:]), jnp.bfloat16)],
        compiler_params=params(),
    )(*prepared, *[p for p, _ in near])

    away = [(p, (dy - 1, o)) for p, (dy, o) in zip(pieces, layout) if dy]
    operands = (*prepared, own, beam, *[p for p, _ in away], vis)
    return pl.pallas_call(
        functools.partial(other_kernel, [place for _, place in away]),
        grid=(slots - 1,),
        out_shape=(vis, jax.ShapeDtypeStruct((integs, 1, share), jnp.float32)),
        in_specs=[IN_VMEM] * (len(operands) - 1) + [pl.BlockSpec(memory_space=pl.ANY)],
        out_specs=(
            pl.BlockSpec(vis_block, lambda k: (0, k + 1, 0, 0, 0, 0, 0)),
            IN_VMEM,
        ),
        scratch_shapes=[pltpu.VMEM((stations - 1, *block_shape[1:]), jnp.bfloat16)],
        input_output_aliases={len(operands) - 1: 0},
        compiler_params=params(),
    )(*operands)


def exchanged(value, offset, dy):
    channels, stations = lax.axis_size("chan"), lax.axis_size("stn")
    if dy == 0:
        return lax.ppermute(value, "chan", [(c, c ^ offset) for c in range(channels)])
    pairs = [
        ((c ^ offset) * stations + (s + dy) % stations, c * stations + s)
        for c in range(channels)
        for s in range(stations)
    ]
    return lax.ppermute(value, ("chan", "stn"), pairs)


def local(voltages, phase_index, int_lengths, beam_weights):
    stations = lax.axis_size("stn")
    channels, parts, rows, samples = voltages.shape
    far = channels // 4
    kept, given = rotate(voltages, phase_index)
    prepared = prepare(int_lengths, beam_weights, stations, channels * rows, samples)

    both = jnp.stack([kept, exchanged(given, 1, 0)], axis=1)
    both = both.reshape(far, 2, 2, parts, rows, samples)
    arrived = [both[0]] + [exchanged(both[k], 4 * k, 0) for k in range(1, far)]

    def held(dx, ks):
        slabs = [arrived[k][dx] for k in ks]
        return slabs[0] if len(slabs) == 1 else jnp.concatenate(slabs, axis=0)

    every = tuple(range(far))
    pieces, layout = [], []
    for dy in range(1, stations):
        pieces.append(exchanged(held(1, (0,)), 2, dy))
        layout.append((1, dy, (0,)))
    order = (0, far - 1, *range(1, far - 1))
    pieces, waited = lax.optimization_barrier((pieces, [arrived[k] for k in order]))
    arrived = [waited[order.index(k)] for k in every]
    for dy in range(stations):
        for dx in range(2):
            ks = every[1:] if dx and dy else every
            piece = held(dx, ks)
            pieces.append(exchanged(piece, 2 * dx, dy) if dx or dy else piece)
            layout.append((dx, dy, ks))
    layout = [
        (dy, tuple(4 * k + 2 * dx + pair for k in ks for pair in range(2)))
        for dx, dy, ks in layout
    ]
    return finish(
        prepared,
        pieces,
        layout,
        stations // 2 + 1,
        int_lengths.shape[0],
        beam_weights.shape[1] // stations,
        (stations, parts, channels, rows, samples),
    )


def solution(mesh):
    return jax.shard_map(
        local,
        mesh=mesh,
        in_specs=(P(None, None, ("stn", "chan"), None), P(("stn", "chan")), P(), P()),
        out_specs=(P("stn", None, None, "chan", None, None, None), P(None, "chan", "stn")),
        check_vma=False,
    )
```

```python
import functools
import math

import jax
import jax.numpy as jnp
from jax import lax
from jax.experimental import pallas as pl
from jax.experimental.pallas import tpu as pltpu
from jax.sharding import PartitionSpec as P

PHASES = 1024
VMEM_BYTES = 32 * 1024 * 1024
IN_VMEM = pl.BlockSpec(memory_space=pltpu.VMEM)
IN_SMEM = pl.BlockSpec(memory_space=pltpu.SMEM)


def params():
    return pltpu.CompilerParams(vmem_limit_bytes=VMEM_BYTES)


def phasors(turns):
    quarter = PHASES // 4
    quadrant = (turns + quarter // 2) // quarter
    x = (turns - quadrant * quarter).astype(jnp.float32) * (2.0 * math.pi / PHASES)
    xx = x * x
    sine = x * (1.0 + xx * (-1.0 / 6 + xx * (1.0 / 120 + xx * (-1.0 / 5040 + xx * (1.0 / 362880)))))
    cosine = 1.0 + xx * (-0.5 + xx * (1.0 / 24 + xx * (-1.0 / 720 + xx * (1.0 / 40320))))
    odd = (quadrant % 2) == 1
    cos_out = jnp.where(odd, sine, cosine)
    sin_out = jnp.where(odd, cosine, sine)
    cos_out = jnp.where((quadrant == 1) | (quadrant == 2), -cos_out, cos_out)
    sin_out = jnp.where((quadrant == 2) | (quadrant == 3), -sin_out, sin_out)
    return cos_out, sin_out


def rotate_kernel(step_ref, volt_ref, out_ref):
    slots = out_ref.shape[0]
    me = lax.axis_index("chan")
    slot = 2 * lax.broadcasted_iota(jnp.int32, step_ref.shape, 1)
    cosine, sine = phasors((step_ref[...] * jnp.bitwise_xor(slot, me)) % PHASES)
    for i in range(slots):
        c = jnp.bitwise_xor(me, 2 * i)
        cos_c = cosine[:, i : i + 1]
        sin_c = sine[:, i : i + 1]
        real_in = volt_ref[c, 0].astype(jnp.float32)
        imag_in = volt_ref[c, 1].astype(jnp.float32)
        out_ref[i, 0] = (real_in * cos_c + imag_in * sin_c).astype(jnp.bfloat16)
        out_ref[i, 1] = (imag_in * cos_c - real_in * sin_c).astype(jnp.bfloat16)


def rotate(voltages, phase_index):
    channels, parts, rows, samples = voltages.shape
    step = jnp.broadcast_to(phase_index[:, None], (rows, 128 * pl.cdiv(channels, 128)))
    return pl.pallas_call(
        rotate_kernel,
        out_shape=jax.ShapeDtypeStruct((channels // 2, parts, rows, samples), jnp.bfloat16),
        in_specs=[IN_VMEM, IN_VMEM],
        out_specs=IN_VMEM,
        compiler_params=params(),
    )(step, voltages)


def prepare_kernel(length_ref, weight_ref, window_ref, inverse_ref, stacked_ref):
    integs = length_ref.shape[0]
    stations, twice, width = stacked_ref.shape
    share, half = twice // 2, width // 2
    sample = lax.broadcasted_iota(jnp.int32, (1, window_ref.shape[1]), 1)
    window_ref[...] = jnp.zeros(window_ref.shape, jnp.float32)
    start = jnp.int32(0)
    for j in range(integs):
        end = start + length_ref[j]
        window_ref[j : j + 1] = jnp.where((sample >= start) & (sample < end), 1.0, 0.0)
        inverse_ref[j : j + 1] = 1.0 / jnp.full((1, inverse_ref.shape[1]), length_ref[j]).astype(
            jnp.float32
        )
        start = end
    rows = pl.ds(pl.multiple_of(lax.axis_index("stn") * share, share), share)
    for b in range(stations):
        w_real = weight_ref[0, rows, b * half : (b + 1) * half]
        w_imag = weight_ref[1, rows, b * half : (b + 1) * half]
        stacked_ref[b, :share, :half] = w_real
        stacked_ref[b, :share, half:] = -w_imag
        stacked_ref[b, share:, :half] = w_imag
        stacked_ref[b, share:, half:] = w_real


def prepare(int_lengths, beam_weights, stations, block, samples):
    share = beam_weights.shape[1] // stations
    return pl.pallas_call(
        prepare_kernel,
        out_shape=(
            jax.ShapeDtypeStruct((16, samples), jnp.float32),
            jax.ShapeDtypeStruct((int_lengths.shape[0], 128), jnp.float32),
            jax.ShapeDtypeStruct((stations, 2 * share, 2 * block), jnp.bfloat16),
        ),
        in_specs=[IN_SMEM, IN_VMEM],
        out_specs=(IN_VMEM, IN_VMEM, IN_VMEM),
        compiler_params=params(),
    )(int_lengths, beam_weights)


def dot_nt(a, b):
    return lax.dot_general(a, b, (((1,), (1,)), ((), ())), preferred_element_type=jnp.float32)


def assemble(pieces, layout, blocks_ref):
    me = lax.axis_index("chan")
    for piece_ref, (block, offsets) in zip(pieces, layout):
        for i, offset in enumerate(offsets):
            source = jnp.bitwise_xor(me, offset)
            for part in range(piece_ref.shape[1]):
                blocks_ref[block, part, source] = piece_ref[i, part]


def assembled(blocks_ref, block):
    _, parts, channels, rows, samples = blocks_ref.shape
    values = blocks_ref[block].astype(jnp.float32)
    return values.reshape(parts * channels * rows, samples).astype(jnp.bfloat16)


def correlate(own, other, window_ref, inverse_ref, vis_ref):
    integs = vis_ref.shape[2]
    twice = own.shape[0]
    half = twice // 2
    window = window_ref[...].astype(jnp.bfloat16)
    masked = jnp.concatenate([own * window[j : j + 1] for j in range(integs)], axis=0)
    products = dot_nt(masked, other)
    for j in range(integs):
        prod = products[j * twice : (j + 1) * twice]
        inverse = inverse_ref[j : j + 1]
        real = prod[:half, :half] + prod[half:, half:]
        imag = prod[half:, :half] - prod[:half, half:]
        vis_ref[0, 0, j, 0, 0] = (real * inverse).astype(jnp.bfloat16)
        vis_ref[0, 0, j, 0, 1] = (imag * inverse).astype(jnp.bfloat16)


def own_kernel(layout, window_ref, inverse_ref, stacked_ref, *refs):
    pieces, (vis_ref, own_ref, beam_ref, blocks_ref) = refs[:-4], refs[-4:]
    assemble(pieces, layout, blocks_ref)
    own = assembled(blocks_ref, 0)
    own_ref[...] = own
    correlate(own, own, window_ref, inverse_ref, vis_ref)
    beam_ref[...] = jnp.dot(
        stacked_ref[lax.axis_index("stn")], own, preferred_element_type=jnp.float32
    )


def other_kernel(layout, window_ref, inverse_ref, stacked_ref, own_ref, beam_ref, *refs):
    pieces, (vis_ref, power_ref, blocks_ref) = refs[:-4], refs[-3:]
    others = blocks_ref.shape[0]
    integs, _, share = power_ref.shape
    station = lax.axis_index("stn")
    slot = pl.program_id(0)

    @pl.when(slot == 0)
    def _():
        assemble(pieces, layout, blocks_ref)

    correlate(own_ref[...], assembled(blocks_ref, slot), window_ref, inverse_ref, vis_ref)

    @pl.when(slot == pl.num_programs(0) - 1)
    def _():
        beam = beam_ref[...]
        for b in range(others):
            weights = stacked_ref[lax.rem(station + b + 1, others + 1)]
            beam = beam + jnp.dot(
                weights, assembled(blocks_ref, b), preferred_element_type=jnp.float32
            )
        power = beam[:share] * beam[:share] + beam[share:] * beam[share:]
        high = power.astype(jnp.bfloat16)
        low = (power - high.astype(jnp.float32)).astype(jnp.bfloat16)
        window = window_ref[...].astype(jnp.bfloat16)
        summed = dot_nt(window, high) + dot_nt(window, low)
        for j in range(integs):
            power_ref[j] = summed[j : j + 1] * inverse_ref[j : j + 1, :share]


def finish(prepared, pieces, layout, slots, integs, share, block_shape):
    stations, parts, channels, rows, samples = block_shape
    half = channels * rows
    vis = jax.ShapeDtypeStruct((1, slots, integs, 1, 2, half, half), jnp.bfloat16)
    vis_block = (1, 1, integs, 1, 2, half, half)

    near = [(p, (0, o)) for p, (dy, o) in zip(pieces, layout) if dy == 0]
    vis, own, beam = pl.pallas_call(
        functools.partial(own_kernel, [place for _, place in near]),
        grid=(1,),
        out_shape=(
            vis,
            jax.ShapeDtypeStruct((2 * half, samples), jnp.bfloat16),
            jax.ShapeDtypeStruct((2 * share, samples), jnp.float32),
        ),
        in_specs=[IN_VMEM] * (len(prepared) + len(near)),
        out_specs=(
            pl.BlockSpec(vis_block, lambda k: (0, 0, 0, 0, 0, 0, 0)),
            IN_VMEM,
            IN_VMEM,
        ),
        scratch_shapes=[pltpu.VMEM((1, *block_shape[1:]), jnp.bfloat16)],
        compiler_params=params(),
    )(*prepared, *[p for p, _ in near])

    away = [(p, (dy - 1, o)) for p, (dy, o) in zip(pieces, layout) if dy]
    operands = (*prepared, own, beam, *[p for p, _ in away], vis)
    return pl.pallas_call(
        functools.partial(other_kernel, [place for _, place in away]),
        grid=(slots - 1,),
        out_shape=(vis, jax.ShapeDtypeStruct((integs, 1, share), jnp.float32)),
        in_specs=[IN_VMEM] * (len(operands) - 1) + [pl.BlockSpec(memory_space=pl.ANY)],
        out_specs=(
            pl.BlockSpec(vis_block, lambda k: (0, k + 1, 0, 0, 0, 0, 0)),
            IN_VMEM,
        ),
        scratch_shapes=[pltpu.VMEM((stations - 1, *block_shape[1:]), jnp.bfloat16)],
        input_output_aliases={len(operands) - 1: 0},
        compiler_params=params(),
    )(*operands)


def exchanged(value, offset, dy):
    channels, stations = lax.axis_size("chan"), lax.axis_size("stn")
    if dy == 0:
        return lax.ppermute(value, "chan", [(c, c ^ offset) for c in range(channels)])
    pairs = [
        ((c ^ offset) * stations + (s + dy) % stations, c * stations + s)
        for c in range(channels)
        for s in range(stations)
    ]
    return lax.ppermute(value, ("chan", "stn"), pairs)


def local(voltages, phase_index, int_lengths, beam_weights):
    stations = lax.axis_size("stn")
    channels, parts, rows, samples = voltages.shape
    far = channels // 4
    pair_phase, pair_voltages = exchanged(phase_index, 1, 0), exchanged(voltages, 1, 0)
    kept = rotate(voltages.astype(jnp.float32), phase_index)
    swapped = rotate(pair_voltages, pair_phase)
    prepared = prepare(int_lengths, beam_weights, stations, channels * rows, samples)

    both = jnp.stack([kept, swapped], axis=1)
    both = both.reshape(far, 2, 2, parts, rows, samples)
    arrived = [both[0]] + [exchanged(both[k], 4 * k, 0) for k in range(1, far)]

    def held(dx, ks):
        slabs = [arrived[k][dx] for k in ks]
        return slabs[0] if len(slabs) == 1 else jnp.concatenate(slabs, axis=0)

    every = tuple(range(far))
    pieces, layout = [], []
    for dy in range(1, stations):
        pieces.append(exchanged(held(1, (0,)), 2, dy))
        layout.append((1, dy, (0,)))
    order = (0, far - 1, *range(1, far - 1))
    pieces, waited = lax.optimization_barrier((pieces, [arrived[k] for k in order]))
    arrived = [waited[order.index(k)] for k in every]
    for dy in range(stations):
        for dx in range(2):
            ks = every[1:] if dx and dy else every
            piece = held(dx, ks)
            pieces.append(exchanged(piece, 2 * dx, dy) if dx or dy else piece)
            layout.append((dx, dy, ks))
    layout = [
        (dy, tuple(4 * k + 2 * dx + pair for k in ks for pair in range(2)))
        for dx, dy, ks in layout
    ]
    return finish(
        prepared,
        pieces,
        layout,
        stations // 2 + 1,
        int_lengths.shape[0],
        beam_weights.shape[1] // stations,
        (stations, parts, channels, rows, samples),
    )


def solution(mesh):
    return jax.shard_map(
        local,
        mesh=mesh,
        in_specs=(P(None, None, ("stn", "chan"), None), P(("stn", "chan")), P(), P()),
        out_specs=(P("stn", None, None, "chan", None, None, None), P(None, "chan", "stn")),
        check_vma=False,
    )
```

```python
import functools
import math

import jax
import jax.numpy as jnp
from jax import lax
from jax.experimental import pallas as pl
from jax.experimental.pallas import tpu as pltpu
from jax.sharding import PartitionSpec as P

PHASES = 1024
VMEM_BYTES = 32 * 1024 * 1024
PREPARE_FLOPS = 3_000_000_000
IN_VMEM = pl.BlockSpec(memory_space=pltpu.VMEM)
IN_SMEM = pl.BlockSpec(memory_space=pltpu.SMEM)


def params():
    return pltpu.CompilerParams(vmem_limit_bytes=VMEM_BYTES)


def phasors(turns):
    quarter = PHASES // 4
    quadrant = (turns + quarter // 2) // quarter
    x = (turns - quadrant * quarter).astype(jnp.float32) * (2.0 * math.pi / PHASES)
    xx = x * x
    sine = x * (1.0 + xx * (-1.0 / 6 + xx * (1.0 / 120 + xx * (-1.0 / 5040 + xx * (1.0 / 362880)))))
    cosine = 1.0 + xx * (-0.5 + xx * (1.0 / 24 + xx * (-1.0 / 720 + xx * (1.0 / 40320))))
    odd = (quadrant % 2) == 1
    cos_out = jnp.where(odd, sine, cosine)
    sin_out = jnp.where(odd, cosine, sine)
    cos_out = jnp.where((quadrant == 1) | (quadrant == 2), -cos_out, cos_out)
    sin_out = jnp.where((quadrant == 2) | (quadrant == 3), -sin_out, sin_out)
    return cos_out, sin_out


def rotate_kernel(step_ref, volt_ref, out_ref):
    slots = out_ref.shape[0]
    me = lax.axis_index("chan")
    slot = 2 * lax.broadcasted_iota(jnp.int32, step_ref.shape, 1)
    cosine, sine = phasors((step_ref[...] * jnp.bitwise_xor(slot, me)) % PHASES)
    for i in range(slots):
        c = jnp.bitwise_xor(me, 2 * i)
        cos_c = cosine[:, i : i + 1]
        sin_c = sine[:, i : i + 1]
        real_in = volt_ref[c, 0].astype(jnp.float32)
        imag_in = volt_ref[c, 1].astype(jnp.float32)
        out_ref[i, 0] = (real_in * cos_c + imag_in * sin_c).astype(jnp.bfloat16)
        out_ref[i, 1] = (imag_in * cos_c - real_in * sin_c).astype(jnp.bfloat16)


def rotate(voltages, phase_index):
    channels, parts, rows, samples = voltages.shape
    step = jnp.broadcast_to(phase_index[:, None], (rows, 128 * pl.cdiv(channels, 128)))
    return pl.pallas_call(
        rotate_kernel,
        out_shape=jax.ShapeDtypeStruct((channels // 2, parts, rows, samples), jnp.bfloat16),
        in_specs=[IN_VMEM, IN_VMEM],
        out_specs=IN_VMEM,
        compiler_params=params(),
    )(step, voltages)


def prepare_kernel(length_ref, weight_ref, window_ref, inverse_ref, stacked_ref):
    integs = length_ref.shape[0]
    stations, twice, width = stacked_ref.shape
    share, half = twice // 2, width // 2
    sample = lax.broadcasted_iota(jnp.int32, (1, window_ref.shape[1]), 1)
    window_ref[...] = jnp.zeros(window_ref.shape, jnp.float32)
    start = jnp.int32(0)
    for j in range(integs):
        end = start + length_ref[j]
        window_ref[j : j + 1] = jnp.where((sample >= start) & (sample < end), 1.0, 0.0)
        inverse_ref[j : j + 1] = 1.0 / jnp.full((1, inverse_ref.shape[1]), length_ref[j]).astype(
            jnp.float32
        )
        start = end
    rows = pl.ds(pl.multiple_of(lax.axis_index("stn") * share, share), share)
    for b in range(stations):
        w_real = weight_ref[0, rows, b * half : (b + 1) * half]
        w_imag = weight_ref[1, rows, b * half : (b + 1) * half]
        stacked_ref[b, :share, :half] = w_real
        stacked_ref[b, :share, half:] = -w_imag
        stacked_ref[b, share:, :half] = w_imag
        stacked_ref[b, share:, half:] = w_real


def prepare(int_lengths, beam_weights, stations, block, samples):
    share = beam_weights.shape[1] // stations
    return pl.pallas_call(
        prepare_kernel,
        out_shape=(
            jax.ShapeDtypeStruct((16, samples), jnp.float32),
            jax.ShapeDtypeStruct((int_lengths.shape[0], 128), jnp.float32),
            jax.ShapeDtypeStruct((stations, 2 * share, 2 * block), jnp.bfloat16),
        ),
        in_specs=[IN_SMEM, IN_VMEM],
        out_specs=(IN_VMEM, IN_VMEM, IN_VMEM),
        cost_estimate=pl.CostEstimate(flops=PREPARE_FLOPS, transcendentals=0, bytes_accessed=0),
        compiler_params=params(),
    )(int_lengths, beam_weights)


def dot_nt(a, b):
    return lax.dot_general(a, b, (((1,), (1,)), ((), ())), preferred_element_type=jnp.float32)


def assemble(pieces, layout, blocks_ref):
    me = lax.axis_index("chan")
    for piece_ref, (block, offsets) in zip(pieces, layout):
        for i, offset in enumerate(offsets):
            source = jnp.bitwise_xor(me, offset)
            for part in range(piece_ref.shape[1]):
                blocks_ref[block, part, source] = piece_ref[i, part]


def assembled(blocks_ref, block):
    _, parts, channels, rows, samples = blocks_ref.shape
    values = blocks_ref[block].astype(jnp.float32)
    return values.reshape(parts * channels * rows, samples).astype(jnp.bfloat16)


def correlate(masked, other, inverse_ref, vis_ref, slot):
    twice = other.shape[0]
    half = twice // 2
    products = dot_nt(masked, other)
    for j in range(vis_ref.shape[2]):
        prod = products[j * twice : (j + 1) * twice]
        inverse = inverse_ref[j : j + 1]
        real = prod[:half, :half] + prod[half:, half:]
        imag = prod[half:, :half] - prod[:half, half:]
        vis_ref[0, slot, j, 0, 0] = (real * inverse).astype(jnp.bfloat16)
        vis_ref[0, slot, j, 0, 1] = (imag * inverse).astype(jnp.bfloat16)


def finish_kernel(layout, window_ref, inverse_ref, stacked_ref, *refs):
    pieces, (vis_ref, power_ref, blocks_ref) = refs[:-3], refs[-3:]
    stations = blocks_ref.shape[0]
    _, slots, integs = vis_ref.shape[:3]
    share = power_ref.shape[2]
    station = lax.axis_index("stn")
    assemble(pieces, layout, blocks_ref)

    own = assembled(blocks_ref, 0)
    window = window_ref[...].astype(jnp.bfloat16)
    masked = jnp.concatenate([own * window[j : j + 1] for j in range(integs)], axis=0)
    for k in range(slots):
        other = assembled(blocks_ref, k) if k else own
        correlate(masked, other, inverse_ref, vis_ref, k)

    beam = jnp.zeros((2 * share, own.shape[1]), jnp.float32)
    for b in range(stations):
        weights = stacked_ref[lax.rem(station + b, stations)]
        beam = beam + jnp.dot(
            weights, assembled(blocks_ref, b), preferred_element_type=jnp.float32
        )
    power = beam[:share] * beam[:share] + beam[share:] * beam[share:]
    high = power.astype(jnp.bfloat16)
    low = (power - high.astype(jnp.float32)).astype(jnp.bfloat16)
    summed = dot_nt(window, high) + dot_nt(window, low)
    for j in range(integs):
        power_ref[j] = summed[j : j + 1] * inverse_ref[j : j + 1, :share]


def finish(prepared, pieces, layout, slots, integs, share, block_shape):
    stations, parts, channels, rows, samples = block_shape
    half = channels * rows
    return pl.pallas_call(
        functools.partial(finish_kernel, layout),
        out_shape=(
            jax.ShapeDtypeStruct((1, slots, integs, 1, 2, half, half), jnp.bfloat16),
            jax.ShapeDtypeStruct((integs, 1, share), jnp.float32),
        ),
        in_specs=[IN_VMEM] * (len(prepared) + len(pieces)),
        out_specs=(IN_VMEM, IN_VMEM),
        scratch_shapes=[pltpu.VMEM(block_shape, jnp.bfloat16)],
        compiler_params=params(),
    )(*prepared, *pieces)


def exchanged(value, offset, dy):
    channels, stations = lax.axis_size("chan"), lax.axis_size("stn")
    if dy == 0:
        return lax.ppermute(value, "chan", [(c, c ^ offset) for c in range(channels)])
    pairs = [
        ((c ^ offset) * stations + (s + dy) % stations, c * stations + s)
        for c in range(channels)
        for s in range(stations)
    ]
    return lax.ppermute(value, ("chan", "stn"), pairs)


def local(voltages, phase_index, int_lengths, beam_weights):
    stations = lax.axis_size("stn")
    channels, parts, rows, samples = voltages.shape
    far = channels // 4
    pair_phase, pair_voltages = exchanged(phase_index, 1, 0), exchanged(voltages, 1, 0)
    kept = rotate(voltages.astype(jnp.float32), phase_index)
    swapped = rotate(pair_voltages, pair_phase)

    both = jnp.stack([kept, swapped], axis=1)
    both = both.reshape(far, 2, 2, parts, rows, samples)
    arrived = [both[0]] + [exchanged(both[k], 4 * k, 0) for k in range(1, far)]

    def held(dx, ks):
        slabs = [arrived[k][dx] for k in ks]
        return slabs[0] if len(slabs) == 1 else jnp.concatenate(slabs, axis=0)

    every = tuple(range(far))
    pieces, layout = [], []
    for dy in range(1, stations):
        pieces.append(exchanged(held(1, (0,)), 2, dy))
        layout.append((1, dy, (0,)))
    order = (0, far - 1, *range(1, far - 1))
    pieces, waited = lax.optimization_barrier((pieces, [arrived[k] for k in order]))
    arrived = [waited[order.index(k)] for k in every]
    for dy in range(1, stations):
        pieces.append(exchanged(held(1, every[1:]), 2, dy))
        layout.append((1, dy, every[1:]))
    pieces, int_lengths, beam_weights = lax.optimization_barrier(
        (pieces, int_lengths, beam_weights)
    )
    prepared = prepare(int_lengths, beam_weights, stations, channels * rows, samples)
    for dy in range(stations):
        for dx in range(1 if dy else 2):
            piece = held(dx, every)
            pieces.append(exchanged(piece, 2 * dx, dy) if dx or dy else piece)
            layout.append((dx, dy, every))
    layout = [
        (dy, tuple(4 * k + 2 * dx + pair for k in ks for pair in range(2)))
        for dx, dy, ks in layout
    ]
    return finish(
        prepared,
        pieces,
        layout,
        stations // 2 + 1,
        int_lengths.shape[0],
        beam_weights.shape[1] // stations,
        (stations, parts, channels, rows, samples),
    )


def solution(mesh):
    return jax.shard_map(
        local,
        mesh=mesh,
        in_specs=(P(None, None, ("stn", "chan"), None), P(("stn", "chan")), P(), P()),
        out_specs=(P("stn", None, None, "chan", None, None, None), P(None, "chan", "stn")),
        check_vma=False,
    )
```

```python
import functools
import math

import jax
import jax.numpy as jnp
from jax import lax
from jax.experimental import pallas as pl
from jax.experimental.pallas import tpu as pltpu
from jax.sharding import PartitionSpec as P

PHASES = 1024
VMEM_BYTES = 32 * 1024 * 1024
PREPARE_FLOPS = 3_000_000_000
IN_VMEM = pl.BlockSpec(memory_space=pltpu.VMEM)
IN_SMEM = pl.BlockSpec(memory_space=pltpu.SMEM)


def params():
    return pltpu.CompilerParams(vmem_limit_bytes=VMEM_BYTES)


def phasors(turns):
    quarter = PHASES // 4
    quadrant = (turns + quarter // 2) // quarter
    x = (turns - quadrant * quarter).astype(jnp.float32) * (2.0 * math.pi / PHASES)
    xx = x * x
    sine = x * (1.0 + xx * (-1.0 / 6 + xx * (1.0 / 120 + xx * (-1.0 / 5040 + xx * (1.0 / 362880)))))
    cosine = 1.0 + xx * (-0.5 + xx * (1.0 / 24 + xx * (-1.0 / 720 + xx * (1.0 / 40320))))
    odd = (quadrant % 2) == 1
    cos_out = jnp.where(odd, sine, cosine)
    sin_out = jnp.where(odd, cosine, sine)
    cos_out = jnp.where((quadrant == 1) | (quadrant == 2), -cos_out, cos_out)
    sin_out = jnp.where((quadrant == 2) | (quadrant == 3), -sin_out, sin_out)
    return cos_out, sin_out


def rotate_kernel(step_ref, volt_ref, out_ref):
    slots = out_ref.shape[0]
    me = lax.axis_index("chan")
    slot = 2 * lax.broadcasted_iota(jnp.int32, step_ref.shape, 1)
    cosine, sine = phasors((step_ref[...] * jnp.bitwise_xor(slot, me)) % PHASES)
    for i in range(slots):
        c = jnp.bitwise_xor(me, 2 * i)
        cos_c = cosine[:, i : i + 1]
        sin_c = sine[:, i : i + 1]
        real_in = volt_ref[c, 0].astype(jnp.float32)
        imag_in = volt_ref[c, 1].astype(jnp.float32)
        out_ref[i, 0] = (real_in * cos_c + imag_in * sin_c).astype(jnp.bfloat16)
        out_ref[i, 1] = (imag_in * cos_c - real_in * sin_c).astype(jnp.bfloat16)


def rotate(voltages, phase_index):
    channels, parts, rows, samples = voltages.shape
    step = jnp.broadcast_to(phase_index[:, None], (rows, 128 * pl.cdiv(channels, 128)))
    return pl.pallas_call(
        rotate_kernel,
        out_shape=jax.ShapeDtypeStruct((channels // 2, parts, rows, samples), jnp.bfloat16),
        in_specs=[IN_VMEM, IN_VMEM],
        out_specs=IN_VMEM,
        compiler_params=params(),
    )(step, voltages)


def prepare_kernel(length_ref, weight_ref, window_ref, inverse_ref, stacked_ref):
    integs = length_ref.shape[0]
    stations, twice, width = stacked_ref.shape
    share, half = twice // 2, width // 2
    sample = lax.broadcasted_iota(jnp.int32, (1, window_ref.shape[1]), 1)
    window_ref[...] = jnp.zeros(window_ref.shape, jnp.float32)
    start = jnp.int32(0)
    for j in range(integs):
        end = start + length_ref[j]
        window_ref[j : j + 1] = jnp.where((sample >= start) & (sample < end), 1.0, 0.0)
        inverse_ref[j : j + 1] = 1.0 / jnp.full((1, inverse_ref.shape[1]), length_ref[j]).astype(
            jnp.float32
        )
        start = end
    rows = pl.ds(pl.multiple_of(lax.axis_index("stn") * share, share), share)
    for b in range(stations):
        w_real = weight_ref[0, rows, b * half : (b + 1) * half]
        w_imag = weight_ref[1, rows, b * half : (b + 1) * half]
        stacked_ref[b, :share, :half] = w_real
        stacked_ref[b, :share, half:] = -w_imag
        stacked_ref[b, share:, :half] = w_imag
        stacked_ref[b, share:, half:] = w_real


def prepare(int_lengths, beam_weights, stations, block, samples):
    share = beam_weights.shape[1] // stations
    return pl.pallas_call(
        prepare_kernel,
        out_shape=(
            jax.ShapeDtypeStruct((16, samples), jnp.float32),
            jax.ShapeDtypeStruct((int_lengths.shape[0], 128), jnp.float32),
            jax.ShapeDtypeStruct((stations, 2 * share, 2 * block), jnp.bfloat16),
        ),
        in_specs=[IN_SMEM, IN_VMEM],
        out_specs=(IN_VMEM, IN_VMEM, IN_VMEM),
        cost_estimate=pl.CostEstimate(flops=PREPARE_FLOPS, transcendentals=0, bytes_accessed=0),
        compiler_params=params(),
    )(int_lengths, beam_weights)


def dot_nt(a, b):
    return lax.dot_general(a, b, (((1,), (1,)), ((), ())), preferred_element_type=jnp.float32)


def assemble(pieces, layout, blocks_ref):
    me = lax.axis_index("chan")
    for piece_ref, (block, offsets) in zip(pieces, layout):
        for i, offset in enumerate(offsets):
            source = jnp.bitwise_xor(me, offset)
            for part in range(piece_ref.shape[1]):
                blocks_ref[block, part, source] = piece_ref[i, part]


def assembled(blocks_ref, block):
    _, parts, channels, rows, samples = blocks_ref.shape
    values = blocks_ref[block].astype(jnp.float32)
    return values.reshape(parts * channels * rows, samples).astype(jnp.bfloat16)


def correlate(masked, other, inverse_ref, vis_ref, slot):
    twice = other.shape[0]
    half = twice // 2
    products = dot_nt(masked, other)
    for j in range(vis_ref.shape[2]):
        prod = products[j * twice : (j + 1) * twice]
        inverse = inverse_ref[j : j + 1]
        real = prod[:half, :half] + prod[half:, half:]
        imag = prod[half:, :half] - prod[:half, half:]
        vis_ref[0, slot, j, 0, 0] = (real * inverse).astype(jnp.bfloat16)
        vis_ref[0, slot, j, 0, 1] = (imag * inverse).astype(jnp.bfloat16)


def finish_kernel(layout, window_ref, inverse_ref, stacked_ref, *refs):
    pieces, (vis_ref, power_ref, blocks_ref) = refs[:-3], refs[-3:]
    stations = blocks_ref.shape[0]
    _, slots, integs = vis_ref.shape[:3]
    share = power_ref.shape[2]
    station = lax.axis_index("stn")
    assemble(pieces, layout, blocks_ref)

    own = assembled(blocks_ref, 0)
    window = window_ref[...].astype(jnp.bfloat16)
    masked = jnp.concatenate([own * window[j : j + 1] for j in range(integs)], axis=0)
    for k in range(slots):
        other = assembled(blocks_ref, k) if k else own
        correlate(masked, other, inverse_ref, vis_ref, k)

    beam = jnp.zeros((2 * share, own.shape[1]), jnp.float32)
    for b in range(stations):
        weights = stacked_ref[lax.rem(station + b, stations)]
        beam = beam + jnp.dot(
            weights, assembled(blocks_ref, b), preferred_element_type=jnp.float32
        )
    power = beam[:share] * beam[:share] + beam[share:] * beam[share:]
    high = power.astype(jnp.bfloat16)
    low = (power - high.astype(jnp.float32)).astype(jnp.bfloat16)
    summed = dot_nt(window, high) + dot_nt(window, low)
    for j in range(integs):
        power_ref[j] = summed[j : j + 1] * inverse_ref[j : j + 1, :share]


def finish(prepared, pieces, layout, slots, integs, share, block_shape):
    stations, parts, channels, rows, samples = block_shape
    half = channels * rows
    return pl.pallas_call(
        functools.partial(finish_kernel, layout),
        out_shape=(
            jax.ShapeDtypeStruct((1, slots, integs, 1, 2, half, half), jnp.bfloat16),
            jax.ShapeDtypeStruct((integs, 1, share), jnp.float32),
        ),
        in_specs=[IN_VMEM] * (len(prepared) + len(pieces)),
        out_specs=(IN_VMEM, IN_VMEM),
        scratch_shapes=[pltpu.VMEM(block_shape, jnp.bfloat16)],
        compiler_params=params(),
    )(*prepared, *pieces)


def exchanged(value, offset, dy):
    channels, stations = lax.axis_size("chan"), lax.axis_size("stn")
    if dy == 0:
        return lax.ppermute(value, "chan", [(c, c ^ offset) for c in range(channels)])
    pairs = [
        ((c ^ offset) * stations + (s + dy) % stations, c * stations + s)
        for c in range(channels)
        for s in range(stations)
    ]
    return lax.ppermute(value, ("chan", "stn"), pairs)


def local(voltages, phase_index, int_lengths, beam_weights):
    stations = lax.axis_size("stn")
    channels, parts, rows, samples = voltages.shape
    far = channels // 4
    pair_phase, pair_voltages = exchanged(phase_index, 1, 0), exchanged(voltages, 1, 0)
    kept = rotate(voltages.astype(jnp.float32), phase_index)
    swapped = rotate(pair_voltages, pair_phase)

    both = jnp.stack([kept, swapped], axis=1)
    both = both.reshape(far, 2, 2, parts, rows, samples)
    arrived = [both[0]] + [exchanged(both[k], 4 * k, 0) for k in range(1, far)]

    def held(dx, ks):
        slabs = [arrived[k][dx] for k in ks]
        return slabs[0] if len(slabs) == 1 else jnp.concatenate(slabs, axis=0)

    every = tuple(range(far))
    pieces, layout = [], []
    for dy in range(1, stations):
        for dx in (1, 0):
            pieces.append(exchanged(held(dx, (0,)), 2 * dx, dy))
            layout.append((dx, dy, (0,)))
    order = (0, far - 1, *range(1, far - 1))
    waited = lax.optimization_barrier([arrived[k] for k in order])
    arrived = [waited[order.index(k)] for k in every]
    for dy in range(1, stations):
        pieces.append(exchanged(held(1, every[1:]), 2, dy))
        layout.append((1, dy, every[1:]))
    pieces, int_lengths, beam_weights = lax.optimization_barrier(
        (pieces, int_lengths, beam_weights)
    )
    prepared = prepare(int_lengths, beam_weights, stations, channels * rows, samples)
    for dy in range(stations):
        for dx in range(1 if dy else 2):
            ks = every[1:] if dy else every
            piece = held(dx, ks)
            pieces.append(exchanged(piece, 2 * dx, dy) if dx or dy else piece)
            layout.append((dx, dy, ks))
    layout = [
        (dy, tuple(4 * k + 2 * dx + pair for k in ks for pair in range(2)))
        for dx, dy, ks in layout
    ]
    return finish(
        prepared,
        pieces,
        layout,
        stations // 2 + 1,
        int_lengths.shape[0],
        beam_weights.shape[1] // stations,
        (stations, parts, channels, rows, samples),
    )


def solution(mesh):
    return jax.shard_map(
        local,
        mesh=mesh,
        in_specs=(P(None, None, ("stn", "chan"), None), P(("stn", "chan")), P(), P()),
        out_specs=(P("stn", None, None, "chan", None, None, None), P(None, "chan", "stn")),
        check_vma=False,
    )
```

```python
import functools
import math

import jax
import jax.numpy as jnp
from jax import lax
from jax.experimental import pallas as pl
from jax.experimental.pallas import tpu as pltpu
from jax.sharding import PartitionSpec as P

PHASES = 1024
VMEM_BYTES = 32 * 1024 * 1024
PREPARE_FLOPS = 3_000_000_000
IN_VMEM = pl.BlockSpec(memory_space=pltpu.VMEM)
IN_SMEM = pl.BlockSpec(memory_space=pltpu.SMEM)


def params():
    return pltpu.CompilerParams(vmem_limit_bytes=VMEM_BYTES)


def phasors(turns):
    quarter = PHASES // 4
    quadrant = (turns + quarter // 2) // quarter
    x = (turns - quadrant * quarter).astype(jnp.float32) * (2.0 * math.pi / PHASES)
    xx = x * x
    sine = x * (1.0 + xx * (-1.0 / 6 + xx * (1.0 / 120 + xx * (-1.0 / 5040 + xx * (1.0 / 362880)))))
    cosine = 1.0 + xx * (-0.5 + xx * (1.0 / 24 + xx * (-1.0 / 720 + xx * (1.0 / 40320))))
    odd = (quadrant % 2) == 1
    cos_out = jnp.where(odd, sine, cosine)
    sin_out = jnp.where(odd, cosine, sine)
    cos_out = jnp.where((quadrant == 1) | (quadrant == 2), -cos_out, cos_out)
    sin_out = jnp.where((quadrant == 2) | (quadrant == 3), -sin_out, sin_out)
    return cos_out, sin_out


def rotate_kernel(stride, step_ref, volt_ref, out_ref):
    slots = out_ref.shape[0]
    me = lax.axis_index("chan")
    slot = 2 * lax.broadcasted_iota(jnp.int32, step_ref.shape, 1)
    cosine, sine = phasors((step_ref[...] * jnp.bitwise_xor(slot, me)) % PHASES)
    for i in range(slots):
        c = jnp.bitwise_xor(me, 2 * i) // stride
        cos_c = cosine[:, i : i + 1]
        sin_c = sine[:, i : i + 1]
        real_in = volt_ref[c, 0].astype(jnp.float32)
        imag_in = volt_ref[c, 1].astype(jnp.float32)
        out_ref[i, 0] = (real_in * cos_c + imag_in * sin_c).astype(jnp.bfloat16)
        out_ref[i, 1] = (imag_in * cos_c - real_in * sin_c).astype(jnp.bfloat16)


def rotate(voltages, phase_index, channels):
    held, parts, rows, samples = voltages.shape
    step = jnp.broadcast_to(phase_index[:, None], (rows, 128 * pl.cdiv(channels, 128)))
    return pl.pallas_call(
        functools.partial(rotate_kernel, channels // held),
        out_shape=jax.ShapeDtypeStruct((channels // 2, parts, rows, samples), jnp.bfloat16),
        in_specs=[IN_VMEM, IN_VMEM],
        out_specs=IN_VMEM,
        compiler_params=params(),
    )(step, voltages)


def prepare_kernel(length_ref, weight_ref, window_ref, inverse_ref, stacked_ref):
    integs = length_ref.shape[0]
    stations, twice, width = stacked_ref.shape
    share, half = twice // 2, width // 2
    sample = lax.broadcasted_iota(jnp.int32, (1, window_ref.shape[1]), 1)
    window_ref[...] = jnp.zeros(window_ref.shape, jnp.float32)
    start = jnp.int32(0)
    for j in range(integs):
        end = start + length_ref[j]
        window_ref[j : j + 1] = jnp.where((sample >= start) & (sample < end), 1.0, 0.0)
        inverse_ref[j : j + 1] = 1.0 / jnp.full((1, inverse_ref.shape[1]), length_ref[j]).astype(
            jnp.float32
        )
        start = end
    rows = pl.ds(pl.multiple_of(lax.axis_index("stn") * share, share), share)
    for b in range(stations):
        w_real = weight_ref[0, rows, b * half : (b + 1) * half]
        w_imag = weight_ref[1, rows, b * half : (b + 1) * half]
        stacked_ref[b, :share, :half] = w_real
        stacked_ref[b, :share, half:] = -w_imag
        stacked_ref[b, share:, :half] = w_imag
        stacked_ref[b, share:, half:] = w_real


def prepare(int_lengths, beam_weights, stations, block, samples):
    share = beam_weights.shape[1] // stations
    return pl.pallas_call(
        prepare_kernel,
        out_shape=(
            jax.ShapeDtypeStruct((16, samples), jnp.float32),
            jax.ShapeDtypeStruct((int_lengths.shape[0], 128), jnp.float32),
            jax.ShapeDtypeStruct((stations, 2 * share, 2 * block), jnp.bfloat16),
        ),
        in_specs=[IN_SMEM, IN_VMEM],
        out_specs=(IN_VMEM, IN_VMEM, IN_VMEM),
        cost_estimate=pl.CostEstimate(flops=PREPARE_FLOPS, transcendentals=0, bytes_accessed=0),
        compiler_params=params(),
    )(int_lengths, beam_weights)


def dot_nt(a, b):
    return lax.dot_general(a, b, (((1,), (1,)), ((), ())), preferred_element_type=jnp.float32)


def assemble(pieces, layout, blocks_ref):
    me = lax.axis_index("chan")
    for piece_ref, (block, offsets) in zip(pieces, layout):
        for i, offset in enumerate(offsets):
            source = jnp.bitwise_xor(me, offset)
            for part in range(piece_ref.shape[1]):
                blocks_ref[block, part, source] = piece_ref[i, part]


def assembled(blocks_ref, block):
    _, parts, channels, rows, samples = blocks_ref.shape
    values = blocks_ref[block].astype(jnp.float32)
    return values.reshape(parts * channels * rows, samples).astype(jnp.bfloat16)


def correlate(masked, other, inverse_ref, vis_ref, slot):
    twice = other.shape[0]
    half = twice // 2
    products = dot_nt(masked, other)
    for j in range(vis_ref.shape[2]):
        prod = products[j * twice : (j + 1) * twice]
        inverse = inverse_ref[j : j + 1]
        real = prod[:half, :half] + prod[half:, half:]
        imag = prod[half:, :half] - prod[:half, half:]
        vis_ref[0, slot, j, 0, 0] = (real * inverse).astype(jnp.bfloat16)
        vis_ref[0, slot, j, 0, 1] = (imag * inverse).astype(jnp.bfloat16)


def finish_kernel(layout, window_ref, inverse_ref, stacked_ref, *refs):
    pieces, (vis_ref, power_ref, blocks_ref) = refs[:-3], refs[-3:]
    stations = blocks_ref.shape[0]
    _, slots, integs = vis_ref.shape[:3]
    share = power_ref.shape[2]
    station = lax.axis_index("stn")
    assemble(pieces, layout, blocks_ref)

    own = assembled(blocks_ref, 0)
    window = window_ref[...].astype(jnp.bfloat16)
    masked = jnp.concatenate([own * window[j : j + 1] for j in range(integs)], axis=0)
    for k in range(slots):
        other = assembled(blocks_ref, k) if k else own
        correlate(masked, other, inverse_ref, vis_ref, k)

    beam = jnp.zeros((2 * share, own.shape[1]), jnp.float32)
    for b in range(stations):
        weights = stacked_ref[lax.rem(station + b, stations)]
        beam = beam + jnp.dot(
            weights, assembled(blocks_ref, b), preferred_element_type=jnp.float32
        )
    power = beam[:share] * beam[:share] + beam[share:] * beam[share:]
    high = power.astype(jnp.bfloat16)
    low = (power - high.astype(jnp.float32)).astype(jnp.bfloat16)
    summed = dot_nt(window, high) + dot_nt(window, low)
    for j in range(integs):
        power_ref[j] = summed[j : j + 1] * inverse_ref[j : j + 1, :share]


def finish(prepared, pieces, layout, slots, integs, share, block_shape):
    stations, parts, channels, rows, samples = block_shape
    half = channels * rows
    return pl.pallas_call(
        functools.partial(finish_kernel, layout),
        out_shape=(
            jax.ShapeDtypeStruct((1, slots, integs, 1, 2, half, half), jnp.bfloat16),
            jax.ShapeDtypeStruct((integs, 1, share), jnp.float32),
        ),
        in_specs=[IN_VMEM] * (len(prepared) + len(pieces)),
        out_specs=(IN_VMEM, IN_VMEM),
        scratch_shapes=[pltpu.VMEM(block_shape, jnp.bfloat16)],
        compiler_params=params(),
    )(*prepared, *pieces)


def exchanged(value, offset, dy):
    channels, stations = lax.axis_size("chan"), lax.axis_size("stn")
    if dy == 0:
        return lax.ppermute(value, "chan", [(c, c ^ offset) for c in range(channels)])
    pairs = [
        ((c ^ offset) * stations + (s + dy) % stations, c * stations + s)
        for c in range(channels)
        for s in range(stations)
    ]
    return lax.ppermute(value, ("chan", "stn"), pairs)


def local(voltages, phase_index, int_lengths, beam_weights):
    stations = lax.axis_size("stn")
    channels, parts, rows, samples = voltages.shape
    far = channels // 4
    pair_phase, pair_voltages = exchanged(phase_index, 1, 0), exchanged(voltages, 1, 0)
    sides = voltages.reshape(channels // 2, 2, parts, rows, samples)
    side = lax.axis_index("chan") % 2
    mine = lax.dynamic_index_in_dim(sides, side, 1, keepdims=False)
    kept = rotate(mine.astype(jnp.float32), phase_index, channels)
    swapped = rotate(pair_voltages, pair_phase, channels)

    both = jnp.stack([kept, swapped], axis=1)
    both = both.reshape(far, 2, 2, parts, rows, samples)
    arrived = [both[0]] + [exchanged(both[k], 4 * k, 0) for k in range(1, far)]

    def held(dx, ks):
        slabs = [arrived[k][dx] for k in ks]
        return slabs[0] if len(slabs) == 1 else jnp.concatenate(slabs, axis=0)

    every = tuple(range(far))
    pieces, layout = [], []
    for dy in range(1, stations):
        pieces.append(exchanged(held(1, (0,)), 2, dy))
        layout.append((1, dy, (0,)))
    order = (0, far - 1, *range(1, far - 1))
    pieces, waited = lax.optimization_barrier((pieces, [arrived[k] for k in order]))
    arrived = [waited[order.index(k)] for k in every]
    for dy in range(1, stations):
        pieces.append(exchanged(held(1, every[1:]), 2, dy))
        layout.append((1, dy, every[1:]))
    pieces, int_lengths, beam_weights = lax.optimization_barrier(
        (pieces, int_lengths, beam_weights)
    )
    prepared = prepare(int_lengths, beam_weights, stations, channels * rows, samples)
    for dy in range(stations):
        for dx in range(1 if dy else 2):
            piece = held(dx, every)
            pieces.append(exchanged(piece, 2 * dx, dy) if dx or dy else piece)
            layout.append((dx, dy, every))
    layout = [
        (dy, tuple(4 * k + 2 * dx + pair for k in ks for pair in range(2)))
        for dx, dy, ks in layout
    ]
    return finish(
        prepared,
        pieces,
        layout,
        stations // 2 + 1,
        int_lengths.shape[0],
        beam_weights.shape[1] // stations,
        (stations, parts, channels, rows, samples),
    )


def solution(mesh):
    return jax.shard_map(
        local,
        mesh=mesh,
        in_specs=(P(None, None, ("stn", "chan"), None), P(("stn", "chan")), P(), P()),
        out_specs=(P("stn", None, None, "chan", None, None, None), P(None, "chan", "stn")),
        check_vma=False,
    )
```

```python
import functools
import math

import jax
import jax.numpy as jnp
from jax import lax
from jax.experimental import pallas as pl
from jax.experimental.pallas import tpu as pltpu
from jax.sharding import PartitionSpec as P

PHASES = 1024
VMEM_BYTES = 32 * 1024 * 1024
PREPARE_FLOPS = 3_000_000_000
IN_VMEM = pl.BlockSpec(memory_space=pltpu.VMEM)
IN_SMEM = pl.BlockSpec(memory_space=pltpu.SMEM)


def params():
    return pltpu.CompilerParams(vmem_limit_bytes=VMEM_BYTES)


def phasors(turns):
    quarter = PHASES // 4
    quadrant = (turns + quarter // 2) // quarter
    x = (turns - quadrant * quarter).astype(jnp.float32) * (2.0 * math.pi / PHASES)
    xx = x * x
    sine = x * (1.0 + xx * (-1.0 / 6 + xx * (1.0 / 120 + xx * (-1.0 / 5040 + xx * (1.0 / 362880)))))
    cosine = 1.0 + xx * (-0.5 + xx * (1.0 / 24 + xx * (-1.0 / 720 + xx * (1.0 / 40320))))
    odd = (quadrant % 2) == 1
    cos_out = jnp.where(odd, sine, cosine)
    sin_out = jnp.where(odd, cosine, sine)
    cos_out = jnp.where((quadrant == 1) | (quadrant == 2), -cos_out, cos_out)
    sin_out = jnp.where((quadrant == 2) | (quadrant == 3), -sin_out, sin_out)
    return cos_out, sin_out


def rotate_kernel(step_ref, volt_ref, out_ref):
    slots = out_ref.shape[0]
    me = lax.axis_index("chan")
    slot = 2 * lax.broadcasted_iota(jnp.int32, step_ref.shape, 1)
    cosine, sine = phasors((step_ref[...] * jnp.bitwise_xor(slot, me)) % PHASES)
    for i in range(slots):
        c = jnp.bitwise_xor(me, 2 * i)
        cos_c = cosine[:, i : i + 1]
        sin_c = sine[:, i : i + 1]
        real_in = volt_ref[c, 0].astype(jnp.float32)
        imag_in = volt_ref[c, 1].astype(jnp.float32)
        out_ref[i, 0] = (real_in * cos_c + imag_in * sin_c).astype(jnp.bfloat16)
        out_ref[i, 1] = (imag_in * cos_c - real_in * sin_c).astype(jnp.bfloat16)


def rotate(voltages, phase_index):
    channels, parts, rows, samples = voltages.shape
    step = jnp.broadcast_to(phase_index[:, None], (rows, 128 * pl.cdiv(channels, 128)))
    return pl.pallas_call(
        rotate_kernel,
        out_shape=jax.ShapeDtypeStruct((channels // 2, parts, rows, samples), jnp.bfloat16),
        in_specs=[IN_VMEM, IN_VMEM],
        out_specs=IN_VMEM,
        compiler_params=params(),
    )(step, voltages)


def prepare_kernel(length_ref, weight_ref, window_ref, inverse_ref, stacked_ref):
    integs = length_ref.shape[0]
    stations, twice, width = stacked_ref.shape
    share, half = twice // 2, width // 2
    sample = lax.broadcasted_iota(jnp.int32, (1, window_ref.shape[1]), 1)
    window_ref[...] = jnp.zeros(window_ref.shape, jnp.float32)
    start = jnp.int32(0)
    for j in range(integs):
        end = start + length_ref[j]
        window_ref[j : j + 1] = jnp.where((sample >= start) & (sample < end), 1.0, 0.0)
        inverse_ref[j : j + 1] = 1.0 / jnp.full((1, inverse_ref.shape[1]), length_ref[j]).astype(
            jnp.float32
        )
        start = end
    rows = pl.ds(pl.multiple_of(lax.axis_index("stn") * share, share), share)
    for b in range(stations):
        w_real = weight_ref[0, rows, b * half : (b + 1) * half]
        w_imag = weight_ref[1, rows, b * half : (b + 1) * half]
        stacked_ref[b, :share, :half] = w_real
        stacked_ref[b, :share, half:] = -w_imag
        stacked_ref[b, share:, :half] = w_imag
        stacked_ref[b, share:, half:] = w_real


def prepare(int_lengths, beam_weights, stations, block, samples):
    share = beam_weights.shape[1] // stations
    return pl.pallas_call(
        prepare_kernel,
        out_shape=(
            jax.ShapeDtypeStruct((16, samples), jnp.float32),
            jax.ShapeDtypeStruct((int_lengths.shape[0], 128), jnp.float32),
            jax.ShapeDtypeStruct((stations, 2 * share, 2 * block), jnp.bfloat16),
        ),
        in_specs=[IN_SMEM, IN_VMEM],
        out_specs=(IN_VMEM, IN_VMEM, IN_VMEM),
        cost_estimate=pl.CostEstimate(flops=PREPARE_FLOPS, transcendentals=0, bytes_accessed=0),
        compiler_params=params(),
    )(int_lengths, beam_weights)


def dot_nt(a, b):
    return lax.dot_general(a, b, (((1,), (1,)), ((), ())), preferred_element_type=jnp.float32)


def assemble(pieces, layout, blocks_ref):
    me = lax.axis_index("chan")
    for piece_ref, (block, offsets) in zip(pieces, layout):
        for i, offset in enumerate(offsets):
            source = jnp.bitwise_xor(me, offset)
            for part in range(piece_ref.shape[1]):
                blocks_ref[block, part, source] = piece_ref[i, part]


def assembled(blocks_ref, block):
    _, parts, channels, rows, samples = blocks_ref.shape
    values = blocks_ref[block].astype(jnp.float32)
    return values.reshape(parts * channels * rows, samples).astype(jnp.bfloat16)


def correlate(masked, other, inverse_ref, vis_ref, slot):
    twice = other.shape[0]
    half = twice // 2
    products = dot_nt(masked, other)
    for j in range(vis_ref.shape[2]):
        prod = products[j * twice : (j + 1) * twice]
        inverse = inverse_ref[j : j + 1]
        real = prod[:half, :half] + prod[half:, half:]
        imag = prod[half:, :half] - prod[:half, half:]
        vis_ref[0, slot, j, 0, 0] = (real * inverse).astype(jnp.bfloat16)
        vis_ref[0, slot, j, 0, 1] = (imag * inverse).astype(jnp.bfloat16)


def finish_kernel(layout, window_ref, inverse_ref, stacked_ref, *refs):
    pieces, (vis_ref, power_ref, blocks_ref) = refs[:-3], refs[-3:]
    stations = blocks_ref.shape[0]
    _, slots, integs = vis_ref.shape[:3]
    share = power_ref.shape[2]
    station = lax.axis_index("stn")
    assemble(pieces, layout, blocks_ref)

    own = assembled(blocks_ref, 0)
    window = window_ref[...].astype(jnp.bfloat16)
    masked = jnp.concatenate([own * window[j : j + 1] for j in range(integs)], axis=0)
    for k in range(slots):
        other = assembled(blocks_ref, k) if k else own
        correlate(masked, other, inverse_ref, vis_ref, k)

    beam = jnp.zeros((2 * share, own.shape[1]), jnp.float32)
    for b in range(stations):
        weights = stacked_ref[lax.rem(station + b, stations)]
        beam = beam + jnp.dot(
            weights, assembled(blocks_ref, b), preferred_element_type=jnp.float32
        )
    power = beam[:share] * beam[:share] + beam[share:] * beam[share:]
    high = power.astype(jnp.bfloat16)
    low = (power - high.astype(jnp.float32)).astype(jnp.bfloat16)
    summed = dot_nt(window, high) + dot_nt(window, low)
    for j in range(integs):
        power_ref[j] = summed[j : j + 1] * inverse_ref[j : j + 1, :share]


def finish(prepared, pieces, layout, slots, integs, share, block_shape):
    stations, parts, channels, rows, samples = block_shape
    half = channels * rows
    return pl.pallas_call(
        functools.partial(finish_kernel, layout),
        out_shape=(
            jax.ShapeDtypeStruct((1, slots, integs, 1, 2, half, half), jnp.bfloat16),
            jax.ShapeDtypeStruct((integs, 1, share), jnp.float32),
        ),
        in_specs=[IN_VMEM] * (len(prepared) + len(pieces)),
        out_specs=(IN_VMEM, IN_VMEM),
        scratch_shapes=[pltpu.VMEM(block_shape, jnp.bfloat16)],
        compiler_params=params(),
    )(*prepared, *pieces)


def exchanged(value, offset, dy):
    channels, stations = lax.axis_size("chan"), lax.axis_size("stn")
    if dy == 0:
        return lax.ppermute(value, "chan", [(c, c ^ offset) for c in range(channels)])
    pairs = [
        ((c ^ offset) * stations + (s + dy) % stations, c * stations + s)
        for c in range(channels)
        for s in range(stations)
    ]
    return lax.ppermute(value, ("chan", "stn"), pairs)


def local(voltages, phase_index, int_lengths, beam_weights):
    stations = lax.axis_size("stn")
    channels, parts, rows, samples = voltages.shape
    far = channels // 4
    pair_phase, pair_voltages = exchanged(phase_index, 1, 0), exchanged(voltages, 1, 0)
    kept = rotate(voltages.astype(jnp.float32), phase_index)
    swapped = rotate(pair_voltages, pair_phase)

    both = jnp.stack([kept, swapped], axis=1)
    both = both.reshape(far, 2, 2, parts, rows, samples)
    arrived = [both[0]] + [exchanged(both[k], 4 * k, 0) for k in range(1, far)]

    def held(dx, ks):
        slabs = [arrived[k][dx] for k in ks]
        return slabs[0] if len(slabs) == 1 else jnp.concatenate(slabs, axis=0)

    every = tuple(range(far))
    pieces, layout = [], []
    for dy in range(1, stations):
        pieces.append(exchanged(held(1, (0,)), 2, dy))
        layout.append((1, dy, (0,)))
    order = (0, far - 1, *range(1, far - 1))
    waited = lax.optimization_barrier([arrived[k] for k in order])
    arrived = [waited[order.index(k)] for k in every]
    for dy in range(1, stations):
        pieces.append(exchanged(held(1, every[1:]), 2, dy))
        layout.append((1, dy, every[1:]))
    pieces, int_lengths, beam_weights = lax.optimization_barrier(
        (pieces, int_lengths, beam_weights)
    )
    prepared = prepare(int_lengths, beam_weights, stations, channels * rows, samples)
    for dy in range(stations):
        for dx in range(1 if dy else 2):
            piece = held(dx, every)
            pieces.append(exchanged(piece, 2 * dx, dy) if dx or dy else piece)
            layout.append((dx, dy, every))
    layout = [
        (dy, tuple(4 * k + 2 * dx + pair for k in ks for pair in range(2)))
        for dx, dy, ks in layout
    ]
    return finish(
        prepared,
        pieces,
        layout,
        stations // 2 + 1,
        int_lengths.shape[0],
        beam_weights.shape[1] // stations,
        (stations, parts, channels, rows, samples),
    )


def solution(mesh):
    return jax.shard_map(
        local,
        mesh=mesh,
        in_specs=(P(None, None, ("stn", "chan"), None), P(("stn", "chan")), P(), P()),
        out_specs=(P("stn", None, None, "chan", None, None, None), P(None, "chan", "stn")),
        check_vma=False,
    )
```

```python
import functools
import math

import jax
import jax.numpy as jnp
from jax import lax
from jax.experimental import pallas as pl
from jax.experimental.pallas import tpu as pltpu
from jax.sharding import PartitionSpec as P

PHASES = 1024
VMEM_BYTES = 32 * 1024 * 1024
PREPARE_FLOPS = 3_000_000_000
IN_VMEM = pl.BlockSpec(memory_space=pltpu.VMEM)
IN_SMEM = pl.BlockSpec(memory_space=pltpu.SMEM)


def params():
    return pltpu.CompilerParams(vmem_limit_bytes=VMEM_BYTES)


def phasors(turns):
    quarter = PHASES // 4
    quadrant = (turns + quarter // 2) // quarter
    x = (turns - quadrant * quarter).astype(jnp.float32) * (2.0 * math.pi / PHASES)
    xx = x * x
    sine = x * (1.0 + xx * (-1.0 / 6 + xx * (1.0 / 120 + xx * (-1.0 / 5040 + xx * (1.0 / 362880)))))
    cosine = 1.0 + xx * (-0.5 + xx * (1.0 / 24 + xx * (-1.0 / 720 + xx * (1.0 / 40320))))
    odd = (quadrant % 2) == 1
    cos_out = jnp.where(odd, sine, cosine)
    sin_out = jnp.where(odd, cosine, sine)
    cos_out = jnp.where((quadrant == 1) | (quadrant == 2), -cos_out, cos_out)
    sin_out = jnp.where((quadrant == 2) | (quadrant == 3), -sin_out, sin_out)
    return cos_out, sin_out


def rotate_kernel(step_ref, volt_ref, out_ref):
    slots = out_ref.shape[0]
    me = lax.axis_index("chan")
    slot = 2 * lax.broadcasted_iota(jnp.int32, step_ref.shape, 1)
    cosine, sine = phasors((step_ref[...] * jnp.bitwise_xor(slot, me)) % PHASES)
    for i in range(slots):
        c = jnp.bitwise_xor(me, 2 * i)
        cos_c = cosine[:, i : i + 1]
        sin_c = sine[:, i : i + 1]
        real_in = volt_ref[c, 0].astype(jnp.float32)
        imag_in = volt_ref[c, 1].astype(jnp.float32)
        out_ref[i, 0] = (real_in * cos_c + imag_in * sin_c).astype(jnp.bfloat16)
        out_ref[i, 1] = (imag_in * cos_c - real_in * sin_c).astype(jnp.bfloat16)


def rotate(voltages, phase_index):
    channels, parts, rows, samples = voltages.shape
    step = jnp.broadcast_to(phase_index[:, None], (rows, 128 * pl.cdiv(channels, 128)))
    return pl.pallas_call(
        rotate_kernel,
        out_shape=jax.ShapeDtypeStruct((channels // 2, parts, rows, samples), jnp.bfloat16),
        in_specs=[IN_VMEM, IN_VMEM],
        out_specs=IN_VMEM,
        compiler_params=params(),
    )(step, voltages)


def prepare_kernel(length_ref, weight_ref, window_ref, inverse_ref, stacked_ref):
    integs = length_ref.shape[0]
    stations, twice, width = stacked_ref.shape
    share, half = twice // 2, width // 2
    sample = lax.broadcasted_iota(jnp.int32, (1, window_ref.shape[1]), 1)
    window_ref[...] = jnp.zeros(window_ref.shape, jnp.float32)
    start = jnp.int32(0)
    for j in range(integs):
        end = start + length_ref[j]
        window_ref[j : j + 1] = jnp.where((sample >= start) & (sample < end), 1.0, 0.0)
        inverse_ref[j : j + 1] = 1.0 / jnp.full((1, inverse_ref.shape[1]), length_ref[j]).astype(
            jnp.float32
        )
        start = end
    rows = pl.ds(pl.multiple_of(lax.axis_index("stn") * share, share), share)
    for b in range(stations):
        w_real = weight_ref[0, rows, b * half : (b + 1) * half]
        w_imag = weight_ref[1, rows, b * half : (b + 1) * half]
        stacked_ref[b, :share, :half] = w_real
        stacked_ref[b, :share, half:] = -w_imag
        stacked_ref[b, share:, :half] = w_imag
        stacked_ref[b, share:, half:] = w_real


def prepare(int_lengths, beam_weights, stations, block, samples):
    share = beam_weights.shape[1] // stations
    return pl.pallas_call(
        prepare_kernel,
        out_shape=(
            jax.ShapeDtypeStruct((16, samples), jnp.float32),
            jax.ShapeDtypeStruct((int_lengths.shape[0], 128), jnp.float32),
            jax.ShapeDtypeStruct((stations, 2 * share, 2 * block), jnp.bfloat16),
        ),
        in_specs=[IN_SMEM, IN_VMEM],
        out_specs=(IN_VMEM, IN_VMEM, IN_VMEM),
        cost_estimate=pl.CostEstimate(flops=PREPARE_FLOPS, transcendentals=0, bytes_accessed=0),
        compiler_params=params(),
    )(int_lengths, beam_weights)


def dot_nt(a, b):
    return lax.dot_general(a, b, (((1,), (1,)), ((), ())), preferred_element_type=jnp.float32)


def assemble(pieces, layout, blocks_ref):
    me = lax.axis_index("chan")
    for piece_ref, (block, offsets) in zip(pieces, layout):
        for i, offset in enumerate(offsets):
            source = jnp.bitwise_xor(me, offset)
            for part in range(piece_ref.shape[1]):
                blocks_ref[block, part, source] = piece_ref[i, part]


def assembled(blocks_ref, block):
    _, parts, channels, rows, samples = blocks_ref.shape
    values = blocks_ref[block].astype(jnp.float32)
    return values.reshape(parts * channels * rows, samples).astype(jnp.bfloat16)


def correlate(masked, other, inverse_ref, vis_ref, slot):
    twice = other.shape[0]
    half = twice // 2
    products = dot_nt(masked, other)
    for j in range(vis_ref.shape[2]):
        prod = products[j * twice : (j + 1) * twice]
        inverse = inverse_ref[j : j + 1]
        real = prod[:half, :half] + prod[half:, half:]
        imag = prod[half:, :half] - prod[:half, half:]
        vis_ref[0, slot, j, 0, 0] = (real * inverse).astype(jnp.bfloat16)
        vis_ref[0, slot, j, 0, 1] = (imag * inverse).astype(jnp.bfloat16)


def finish_kernel(layout, window_ref, inverse_ref, stacked_ref, *refs):
    pieces, (vis_ref, power_ref, blocks_ref) = refs[:-3], refs[-3:]
    stations = blocks_ref.shape[0]
    _, slots, integs = vis_ref.shape[:3]
    share = power_ref.shape[2]
    station = lax.axis_index("stn")
    assemble(pieces, layout, blocks_ref)

    own = assembled(blocks_ref, 0)
    window = window_ref[...].astype(jnp.bfloat16)
    masked = jnp.concatenate([own * window[j : j + 1] for j in range(integs)], axis=0)
    for k in range(slots):
        other = assembled(blocks_ref, k) if k else own
        correlate(masked, other, inverse_ref, vis_ref, k)

    beam = jnp.zeros((2 * share, own.shape[1]), jnp.float32)
    for b in range(stations):
        weights = stacked_ref[lax.rem(station + b, stations)]
        beam = beam + jnp.dot(
            weights, assembled(blocks_ref, b), preferred_element_type=jnp.float32
        )
    power = beam[:share] * beam[:share] + beam[share:] * beam[share:]
    high = power.astype(jnp.bfloat16)
    low = (power - high.astype(jnp.float32)).astype(jnp.bfloat16)
    summed = dot_nt(window, high) + dot_nt(window, low)
    for j in range(integs):
        power_ref[j] = summed[j : j + 1] * inverse_ref[j : j + 1, :share]


def finish(prepared, pieces, layout, slots, integs, share, block_shape):
    stations, parts, channels, rows, samples = block_shape
    half = channels * rows
    return pl.pallas_call(
        functools.partial(finish_kernel, layout),
        out_shape=(
            jax.ShapeDtypeStruct((1, slots, integs, 1, 2, half, half), jnp.bfloat16),
            jax.ShapeDtypeStruct((integs, 1, share), jnp.float32),
        ),
        in_specs=[IN_VMEM] * (len(prepared) + len(pieces)),
        out_specs=(IN_VMEM, IN_VMEM),
        scratch_shapes=[pltpu.VMEM(block_shape, jnp.bfloat16)],
        compiler_params=params(),
    )(*prepared, *pieces)


def exchanged(value, offset, dy):
    channels, stations = lax.axis_size("chan"), lax.axis_size("stn")
    if dy == 0:
        return lax.ppermute(value, "chan", [(c, c ^ offset) for c in range(channels)])
    pairs = [
        ((c ^ offset) * stations + (s + dy) % stations, c * stations + s)
        for c in range(channels)
        for s in range(stations)
    ]
    return lax.ppermute(value, ("chan", "stn"), pairs)


def local(voltages, phase_index, int_lengths, beam_weights):
    stations = lax.axis_size("stn")
    channels, parts, rows, samples = voltages.shape
    far = channels // 4
    pair_phase, pair_voltages = exchanged(phase_index, 1, 0), exchanged(voltages, 1, 0)
    kept = rotate(voltages.astype(jnp.float32), phase_index)
    swapped = rotate(pair_voltages, pair_phase)

    both = jnp.stack([kept, swapped], axis=1)
    both = both.reshape(far, 2, 2, parts, rows, samples)
    arrived = [both[0]] + [exchanged(both[k], 4 * k, 0) for k in range(1, far)]

    def held(dx, ks):
        slabs = [arrived[k][dx] for k in ks]
        return slabs[0] if len(slabs) == 1 else jnp.concatenate(slabs, axis=0)

    every = tuple(range(far))
    pieces, layout = [], []
    for dy in range(1, stations):
        for dx in (1, 0):
            pieces.append(exchanged(held(dx, (0,)), 2 * dx, dy))
            layout.append((dx, dy, (0,)))
    pieces.append(exchanged(held(1, (0,)), 2, 0))
    layout.append((1, 0, (0,)))
    order = (0, far - 1, *range(1, far - 1))
    waited = lax.optimization_barrier([arrived[k] for k in order])
    arrived = [waited[order.index(k)] for k in every]
    for dy in range(1, stations):
        pieces.append(exchanged(held(1, every[1:]), 2, dy))
        layout.append((1, dy, every[1:]))
    pieces, int_lengths, beam_weights = lax.optimization_barrier(
        (pieces, int_lengths, beam_weights)
    )
    prepared = prepare(int_lengths, beam_weights, stations, channels * rows, samples)
    for dy in range(stations):
        for dx in range(1 if dy else 2):
            ks = every[1:] if dx or dy else every
            piece = held(dx, ks)
            pieces.append(exchanged(piece, 2 * dx, dy) if dx or dy else piece)
            layout.append((dx, dy, ks))
    layout = [
        (dy, tuple(4 * k + 2 * dx + pair for k in ks for pair in range(2)))
        for dx, dy, ks in layout
    ]
    return finish(
        prepared,
        pieces,
        layout,
        stations // 2 + 1,
        int_lengths.shape[0],
        beam_weights.shape[1] // stations,
        (stations, parts, channels, rows, samples),
    )


def solution(mesh):
    return jax.shard_map(
        local,
        mesh=mesh,
        in_specs=(P(None, None, ("stn", "chan"), None), P(("stn", "chan")), P(), P()),
        out_specs=(P("stn", None, None, "chan", None, None, None), P(None, "chan", "stn")),
        check_vma=False,
    )
```
